128 devices in a mesh: gx: 32 (over x, y, core), gy: 4 (over z).
Axes of the slice: x: 4, y: 4, z: 4, core: 2. Of those that a mesh axis runs over, the one named last changes fastest.
Arguments:
- coarse: bfloat16 [32, 4, 8, 64, 128], P('gx', 'gy'), may hold values from -6 to 6
- lists: int32 [32, 4, 4], P('gx', 'gy'), may hold values from 0 to 1023, as said below
- interp: bfloat16 [1024, 256, 4, 128], P('gx', 'gy'), may hold values from -0.25 to 0.25
- fine_own: bfloat16 [1024, 256, 128], P('gx', 'gy'), may hold values from -6 to 6
- lift: bfloat16 [64, 128], replicated, may hold values from -0.75 to 0.75
- conv_a: bfloat16 [9, 128, 128], replicated, may hold values from -0.1875 to 0.1875
- conv_b: bfloat16 [9, 128, 128], replicated, may hold values from -0.1875 to 0.1875
- cotangent: bfloat16 [1024, 256, 128], P('gx', 'gy'), may hold values from -8 to 8
Outputs:
- output: bfloat16 [1024, 256, 128], P('gx', 'gy')
- grad_conv_a: float32 [9, 128, 128], P(None, None, 'gx')
- grad_conv_b: float32 [9, 128, 128], P(None, None, 'gx')
- grad_coarse: float32 [32, 4, 8, 64, 128], P('gx', 'gy')
The draws below stay inside these ranges and needn't reach their ends.
Inputs may be any that keep to these rules, and one draw needn't show every extreme that they name: `lists`: each id names a block of the tile's own coarse tile or of a coarse tile adjacent to it along either or both dimensions.
All inputs are finite; a program needn't handle non-finite values.
Results may differ from the reference program's by a relative error of at most 0.0065.
Values may be sent and summed in bfloat16 or wider, within the bound.
A program may use at most 64 MiB of HBM per device.

```python
import jax
import jax.numpy as jnp
from jax import lax

C = 128
CIN = 64
CELLS = 128
K = 4
TAPS = 9
CB_DEV = 8
FX_DEV = 32
FY_DEV = 64
TX = 32
TY = 4
NFX = 1024
NFY = 256


def draw_lists(key, part):
    key = jax.random.fold_in(key, 7)
    first_key, second_key, third_key = jax.random.split(key, 3)
    along_x = jnp.arange(TX, dtype=jnp.int32)[:, None, None]
    along_y = jnp.arange(TY, dtype=jnp.int32)[None, :, None]
    owner_x = jnp.clip(along_x + jax.random.randint(first_key, (TX, TY, K), -1, 2), 0, TX - 1)
    owner_y = jnp.clip(along_y + jax.random.randint(second_key, (TX, TY, K), -1, 2), 0, TY - 1)
    within = jax.random.randint(third_key, (TX, TY, K), 0, CB_DEV)
    ids = (owner_x * TY + owner_y) * CB_DEV + within
    leading = (jnp.arange(K, dtype=jnp.int32) == 0)[None, None, :]
    top_tile = (along_x == TX - 1) & (along_y == TY - 1) & leading
    low_tile = (along_x == 0) & (along_y == 0) & leading
    ids = jnp.where(top_tile, TX * TY * CB_DEV - 1, ids)
    ids = jnp.where(low_tile, 0, ids)
    return ids.astype(jnp.int32)


def with_spikes(result, rng, source, target, blocks, factor):
    owner, partner = [(jnp.arange(result.shape[dim]) // (result.shape[dim] // blocks)).reshape([-1 if axis == dim else 1 for axis in range(result.ndim)]) for dim in (source, target)]
    chosen = jax.random.permutation(rng, blocks)[partner]
    strong = (owner == chosen) | (owner == (partner + blocks // 2) % blocks)
    return jnp.where(strong, factor * result, result)


def level_of(key, shape, cuts, low, largest):
    loudness, own = 1.0, jax.random.fold_in(key, 6)
    for dim, blocks in cuts:
        steps = jnp.exp(jax.random.uniform(jax.random.fold_in(own, dim), (blocks,), jnp.float32, low / len(cuts), largest / len(cuts)))
        loudness = loudness * jnp.repeat(steps, shape[dim] // blocks).reshape([-1 if axis == dim else 1 for axis in range(len(shape))])
    return loudness


def gaussian(stream_key, dims, scale, reach, cuts=(), held_as=jnp.bfloat16):
    gain = level_of(stream_key, dims, cuts, -0.22, 0.18) if cuts else 1.0
    drawn = jax.random.normal(stream_key, dims, jnp.float32) * scale * gain
    return jnp.minimum(jnp.maximum(drawn, -reach), reach).astype(held_as)


def bell_draw_with(key, shape, spread, most, shards, heavy, kind=jnp.bfloat16):
    drawn = spread * jax.random.normal(key, shape, jnp.float32)
    if shards:
        drawn = drawn * level_of(key, shape, shards, -0.22, 0.18)
    return jnp.clip(with_spikes(drawn, jax.random.fold_in(key, 3), *heavy), -most, most).astype(kind)


def setup_inputs(seed: int = 0) -> dict:
    arg_keys = jax.random.split(jax.random.key(seed), 9)
    coarse = gaussian(arg_keys[0], (TX, TY, CB_DEV, CIN, CELLS), 1.0, 6.0, ((0, 32), (1, 4)))
    lists = draw_lists(jax.random.fold_in(arg_keys[8], 71), 0)
    interp = gaussian(arg_keys[2], (NFX, NFY, K, CELLS), (K * CELLS) ** -0.5, 0.25, ((0, 32), (1, 4)))
    fine_own = gaussian(arg_keys[3], (NFX, NFY, C), 1.0, 6.0, ((0, 32), (1, 4)))
    lift = gaussian(arg_keys[4], (CIN, C), CIN ** -0.5, 0.75)
    conv_a = gaussian(arg_keys[5], (TAPS, C, C), (TAPS * C) ** -0.5, 0.1875)
    conv_b = gaussian(arg_keys[6], (TAPS, C, C), (TAPS * C) ** -0.5, 0.1875)
    cotangent = bell_draw_with(arg_keys[7], (NFX, NFY, C), 1.0, 8.0, ((0, 32), (1, 4)), (0, 2, 32, 2.75))
    return {"coarse": coarse, "lists": lists, "interp": interp, "fine_own": fine_own, "lift": lift, "conv_a": conv_a, "conv_b": conv_b, "cotangent": cotangent}


def offsets():
    return [(di, dj) for di in (-1, 0, 1) for dj in (-1, 0, 1)]

def conv_valid(padded, weights, rows, cols):
    chans = padded.shape[2]
    total = jnp.zeros((rows * cols, weights.shape[2]), jnp.float32)
    for tap, (di, dj) in enumerate(offsets()):
        piece = padded[1 + di:1 + di + rows, 1 + dj:1 + dj + cols].reshape(-1, chans)
        total = total + jnp.dot(piece, weights[tap], preferred_element_type=jnp.float32)
    return total.reshape(rows, cols, -1)

def conv_back(padded, weights, rows, cols):
    chans = padded.shape[2]
    total = jnp.zeros((rows * cols, weights.shape[1]), jnp.float32)
    for tap, (di, dj) in enumerate(offsets()):
        piece = padded[1 - di:1 - di + rows, 1 - dj:1 - dj + cols].reshape(-1, chans)
        total = total + lax.dot_general(piece, weights[tap], (((1,), (1,)), ((), ())), preferred_element_type=jnp.float32)
    return total.reshape(rows, cols, -1)

def weight_grad(padded, grad):
    rows, cols, chans = grad.shape
    flat = grad.reshape(-1, chans)
    parts = []
    for tap, (di, dj) in enumerate(offsets()):
        piece = padded[1 + di:1 + di + rows, 1 + dj:1 + dj + cols].reshape(-1, padded.shape[2])
        parts.append(lax.dot_general(piece, flat, (((0,), (0,)), ((), ())), preferred_element_type=jnp.float32))
    return jnp.stack(parts)

def pad_one(field):
    return jnp.pad(field, ((1, 1), (1, 1), (0, 0)))

def reference(coarse, lists, interp, fine_own, lift, conv_a, conv_b, cotangent):
    flat_coarse = coarse.reshape(TX * TY * CB_DEV, CIN, CELLS)
    blocks = flat_coarse[lists]
    weights6 = interp.reshape(TX, FX_DEV, TY, FY_DEV, K, CELLS)

    def tile_regrid(pair):
        wts, blk = pair
        return jnp.einsum('xtykc,tkic->xtyi', wts.astype(jnp.float32), blk.astype(jnp.float32)).astype(jnp.bfloat16)
    regrid = lax.map(tile_regrid, (weights6, blocks)).reshape(NFX * NFY, CIN)
    field = fine_own.reshape(-1, C).astype(jnp.float32) + jnp.dot(regrid, lift, preferred_element_type=jnp.float32)
    field = field.astype(jnp.bfloat16).reshape(NFX, NFY, C)
    pre = conv_valid(pad_one(field), conv_a, NFX, NFY)
    act = jax.nn.silu(pre).astype(jnp.bfloat16)
    output = (field.astype(jnp.float32) + conv_valid(pad_one(act), conv_b, NFX, NFY)).astype(jnp.bfloat16)
    grad_conv_b = weight_grad(pad_one(act), cotangent)
    back_act = conv_back(pad_one(cotangent), conv_b, NFX, NFY)
    sig = jax.nn.sigmoid(pre)
    back_pre = (back_act * sig * (1.0 + pre * (1.0 - sig))).astype(jnp.bfloat16)
    grad_conv_a = weight_grad(pad_one(field), back_pre)
    back_field = (cotangent.astype(jnp.float32) + conv_back(pad_one(back_pre), conv_a, NFX, NFY)).astype(jnp.bfloat16)
    back_regrid = lax.dot_general(back_field.reshape(-1, C), lift, (((1,), (1,)), ((), ())), preferred_element_type=jnp.float32).astype(jnp.bfloat16)
    back6 = back_regrid.reshape(TX, FX_DEV, TY, FY_DEV, CIN)

    def tile_adjoint(pair):
        wts, grads = pair
        return jnp.einsum('xtykc,xtyi->tkic', wts.astype(jnp.float32), grads.astype(jnp.float32))
    back_blocks = lax.map(tile_adjoint, (weights6, back6))
    grad_flat = jnp.zeros((TX * TY * CB_DEV, CIN, CELLS), jnp.float32)
    grad_flat = grad_flat.at[lists.reshape(-1)].add(back_blocks.reshape(-1, CIN, CELLS))
    grad_coarse = grad_flat.reshape(TX, TY, CB_DEV, CIN, CELLS)
    return (output, grad_conv_a, grad_conv_b, grad_coarse)
```

```python
import functools

import jax
import jax.numpy as jnp
from jax import lax
from jax.experimental import pallas as pl
from jax.experimental.pallas import tpu as pltpu
from jax.sharding import PartitionSpec as P

MESH = pl.DeviceIdType.MESH
F32 = jnp.float32
BF16 = jnp.bfloat16
MIB = 1024 * 1024
NT = (((1,), (1,)), ((), ()))


class Sizes:
    def __init__(self, gx, gy, nx, ny, rows, cols, chans, chans_in, cells, listed, blocks):
        self.gx, self.gy, self.nx, self.ny = gx, gy, nx, ny
        self.rows, self.cols = rows, cols
        self.chans, self.chans_in, self.cells = chans, chans_in, cells
        self.listed, self.blocks = listed, blocks
        self.px = rows * cols
        self.width = cols + 32
        self.ext = cols + 16
        self.span = chans // gx
        self.pack = -(-3 * self.span // 16) * 16
        self.taps = 9 * chans
        self.ch_main = 4 if rows % 4 == 0 else rows
        self.ch_ext = 2


def kernel(
    sz,
    lists, coarse, interp, fine, lift, wa, wb, cot,
    out, ga, gb, gc,
    call, lvec, lrecv, lsm, picked, crecv,
    raw, rawf, interp2, fine_v, lift_v, wa_v, wb_v, wat, wbt, cot_v, bt,
    x_cot, x_field, x_act, x_bp, a_cot, a_field, a_act, a_bp,
    back_act, field, out_v, cot_t, bp_t,
    hs_cols, hs_corner, hr_rows, hr_cols, hr_corner,
    wsum, wsend, w1, wst2, w2, w3,
    gsum, gsend, g1, g2send, g2, gacc,
    local_sem, lsem, csend, crcv, hsend, hrcv, wsnd, wrcv, gsnd, grcv,
):
    tx = lax.axis_index("gx")
    ty = lax.axis_index("gy")
    gx, gy, nx, ny = sz.gx, sz.gy, sz.nx, sz.ny
    rows, cols, chans, width, ext, px = sz.rows, sz.cols, sz.chans, sz.width, sz.ext, sz.px
    core = tx % 2
    cy = (tx // 2) % ny
    cx = tx // (2 * ny)
    left, right = (tx + gx - 1) % gx, (tx + 1) % gx
    down, up = (ty + gy - 1) % gy, (ty + 1) % gy
    started = []

    def remote(src, dst, ssem, rsem, px_, py_):
        copy = pltpu.make_async_remote_copy(
            src_ref=src, dst_ref=dst, send_sem=ssem, recv_sem=rsem,
            device_id=(px_, py_), device_id_type=MESH,
        )
        copy.start()
        started.append(copy)
        return copy

    def local(src, dst, i):
        copy = pltpu.make_async_copy(src, dst, local_sem.at[i])
        copy.start()
        return copy

    ld_coarse = local(coarse, call.at[1], 0)
    ld_cot = local(cot, cot_v, 1)
    ld_raw = local(interp, raw, 2)
    ld_wb = local(wb, wb_v, 3)
    ld_wa = local(wa, wa_v, 4)
    ld_fine = local(fine, fine_v, 5)
    ld_lift = local(lift, lift_v, 6)

    halo = [(left, ty), (right, ty), (tx, down), (tx, up),
            (left, down), (left, up), (right, down), (right, up)]
    peers = list(halo)
    for o in range(2, gy - 1):
        peers.append((tx, (ty + o) % gy))
    for o in range(1, ny):
        for c in range(2):
            peers.append((((cx * ny + (cy + o) % ny) * 2 + c), ty))
    for o in range(1, nx):
        for c in range(2):
            peers.append(((((cx + o) % nx) * ny + cy) * 2 + c, ty))
    barrier = pltpu.get_barrier_semaphore()
    for p in peers:
        pl.semaphore_signal(barrier, inc=1, device_id=p, device_id_type=MESH)
    rowi = lax.broadcasted_iota(jnp.int32, (8, 128), 0)
    vec = jnp.zeros((8, 128), jnp.int32)
    for k in range(sz.listed):
        vec = jnp.where(rowi == k, lists[0, k], vec)
    lvec[...] = vec
    ld_coarse.wait()
    pl.semaphore_wait(barrier, len(peers))

    c1 = [remote(call.at[1], call.at[2], csend.at[0], crcv.at[0], left, ty),
          remote(call.at[1], call.at[0], csend.at[1], crcv.at[1], right, ty)]
    l1 = [remote(lvec, lrecv.at[1], csend.at[2], crcv.at[2], tx, down),
          remote(lvec, lrecv.at[0], csend.at[3], crcv.at[3], tx, up)]

    def fill(x, src):
        def body(r, _):
            x[pl.ds(pl.multiple_of((r + 2) * width + 16, 16), cols), :] = src[
                pl.ds(pl.multiple_of(r * cols, cols), cols), :].astype(F32)
            return 0
        lax.fori_loop(0, rows, body, 0)

    def rim_send(e, x, main):
        cps = []
        n2 = 2 * cols
        cps.append(remote(main.at[pl.ds(0, n2), :], hr_rows.at[e, 1],
                          hsend.at[e, 0], hrcv.at[e, 0], left, ty))
        cps.append(remote(main.at[pl.ds(px - n2, n2), :], hr_rows.at[e, 0],
                          hsend.at[e, 1], hrcv.at[e, 1], right, ty))
        for s, c0 in ((0, 0), (1, cols - 2)):
            for j in range(2):
                hs_cols[e, s, j * rows:(j + 1) * rows, :] = x[
                    pl.ds(2 * width + 16 + c0 + j, rows, stride=width), :].astype(BF16)
        cps.append(remote(hs_cols.at[e, 0], hr_cols.at[e, 1],
                          hsend.at[e, 2], hrcv.at[e, 2], tx, down))
        cps.append(remote(hs_cols.at[e, 1], hr_cols.at[e, 0],
                          hsend.at[e, 3], hrcv.at[e, 3], tx, up))
        q = 0
        for sr, r0, tox in ((0, 0, left), (1, rows - 2, right)):
            for sc, c0, toy in ((0, 0, down), (1, cols - 2, up)):
                parts = [x[(2 + r0 + i) * width + 16 + c0:(2 + r0 + i) * width + 18 + c0, :]
                         for i in range(2)]
                parts.append(jnp.zeros((12, chans), F32))
                hs_corner[e, q] = jnp.concatenate(parts, axis=0).astype(BF16)
                cps.append(remote(hs_corner.at[e, q], hr_corner.at[e, 3 - q],
                                  hsend.at[e, 4 + q], hrcv.at[e, 4 + q], tox, toy))
                q += 1
        return cps

    in_x = (tx > 0, tx < gx - 1)
    in_y = (ty > 0, ty < gy - 1)

    def rim_take(e, x, cps):
        for cp in cps:
            cp.wait_recv()
        for s, r0 in ((0, 0), (1, rows + 2)):
            v = jnp.where(in_x[s], hr_rows[e, s].astype(F32), 0.0)
            for i in range(2):
                x[(r0 + i) * width + 16:(r0 + i) * width + 16 + cols, :] = v[i * cols:(i + 1) * cols]
        for s, c0 in ((0, 14), (1, 16 + cols)):
            v = jnp.where(in_y[s], hr_cols[e, s].astype(F32), 0.0)
            for j in range(2):
                x[pl.ds(2 * width + c0 + j, rows, stride=width), :] = v[j * rows:(j + 1) * rows]
        q = 0
        for sr, r0 in ((0, 0), (1, rows + 2)):
            for sc, c0 in ((0, 14), (1, 16 + cols)):
                v = jnp.where(jnp.logical_and(in_x[sr], in_y[sc]),
                              hr_corner[e, q].astype(F32), 0.0)
                for i in range(2):
                    x[(r0 + i) * width + c0:(r0 + i) * width + c0 + 2, :] = v[2 * i:2 * i + 2]
                q += 1

    def widen(x, a):
        def body(r, _):
            base = pl.multiple_of(r * width, 16)
            for dj in range(3):
                v = x[pl.ds(base + 15 + dj, cols + 8), :]
                w = x[pl.ds(base + 7 + dj, 8), :]
                a[r, :, dj * chans:(dj + 1) * chans] = jnp.concatenate([v, w], axis=0).astype(BF16)
            return 0
        lax.fori_loop(0, rows + 4, body, 0)

    def widen_main(x, a):
        def body(r, _):
            base = pl.multiple_of((r + 1) * width, 16)
            for dj in range(3):
                a[pl.ds(pl.multiple_of(r * cols, cols), cols), dj * chans:(dj + 1) * chans] = x[
                    pl.ds(base + 15 + dj, cols), :].astype(BF16)
            return 0
        lax.fori_loop(0, rows + 2, body, 0)

    def conv_ext(a, w, r, n):
        v = jnp.concatenate(
            [a[pl.ds(r + d, n)].reshape(n * ext, 3 * chans) for d in range(3)], axis=1)
        return jnp.dot(v, w[...], preferred_element_type=F32)

    def conv_main(a, w, r, n):
        v = jnp.concatenate(
            [a[pl.ds(pl.multiple_of((r + d) * cols, cols), n * cols), :] for d in range(3)], axis=1)
        return jnp.dot(v, w[...], preferred_element_type=F32)

    ld_cot.wait()
    fill(x_cot, cot_v)
    h_cot = rim_send(0, x_cot, cot_v)

    ld_wb.wait()
    ld_wa.wait()
    for src, dst in ((wb_v, wbt), (wa_v, wat)):
        for t in range(9):
            dst[t * chans:(t + 1) * chans, :] = src[
                (8 - t) * chans:(9 - t) * chans, :].astype(F32).T.astype(BF16)

    ld_raw.wait()
    step = px // 8
    listed, cells, chans_in = sz.listed, sz.cells, sz.chans_in

    def relay(i, _):
        rawf[...] = raw[pl.ds(pl.multiple_of(i * step * listed, 16), step * listed), :].astype(F32)
        for k in range(listed):
            interp2[pl.ds(pl.multiple_of(i * step, 16), step), k * cells:(k + 1) * cells] = rawf[
                pl.ds(k, step, stride=listed), :].astype(BF16)
        return 0
    lax.fori_loop(0, 8, relay, 0)

    for cp in c1 + l1:
        cp.wait_recv()
    ld_l = pltpu.make_async_copy(lrecv, lsm, lsem)
    ld_l.start()
    ld_l.wait()

    def clip(v):
        return jnp.minimum(jnp.maximum(v, 0), 2)

    nb = sz.blocks
    c2 = []
    for s, toy in ((0, down), (1, up)):
        for k in range(listed):
            i = lsm[s, k, 0]
            picked[s, k] = call[clip(i // (nb * gy) - tx + 1), i % nb]
        c2.append(remote(picked.at[s], crecv.at[1 - s], csend.at[4 + s], crcv.at[4 + s], tx, toy))
    ids = [lists[0, k] for k in range(listed)]
    for k in range(listed):
        i = ids[k]
        crecv[2, k] = call[clip(i // (nb * gy) - tx + 1), i % nb]

    rim_take(0, x_cot, h_cot)
    widen(x_cot, a_cot)
    ce = sz.ch_ext

    def back_body(i, _):
        back_act[pl.ds(pl.multiple_of(i * (ce * ext), 16), ce * ext), :] = conv_ext(
            a_cot, wbt, i * ce, ce)
        return 0
    lax.fori_loop(0, (rows + 2) // ce, back_body, 0)

    ri = lax.broadcasted_iota(jnp.int32, (chans, chans), 0)
    ci = lax.broadcasted_iota(jnp.int32, (chans, chans), 1)
    span = sz.span

    def order(first, second, first_is_y):
        m, rest = ri // (second * span), ri % (second * span)
        s, j = rest // span, rest % span
        if first_is_y:
            return (s * ny + m // 2) * 2 * span + (m % 2) * span + j
        return ((m // 2) * ny + s) * 2 * span + (m % 2) * span + j

    perm_b = jnp.where(ci == order(ny, nx, True), 1.0, 0.0).astype(BF16)
    perm_a = jnp.where(ci == order(nx, ny, False), 1.0, 0.0).astype(BF16)
    cm = sz.ch_main
    pc = cm * cols

    def turn_cot(i, _):
        q = pl.multiple_of(i * pc, 128)
        cot_t[:, pl.ds(q, pc)] = lax.dot_general(
            perm_b, cot_v[pl.ds(q, pc), :], NT, preferred_element_type=F32).astype(BF16)
        return 0
    lax.fori_loop(0, px // pc, turn_cot, 0)

    for cp in c2:
        cp.wait_recv()
    for k in range(listed):
        oy = (ids[k] // nb) % gy
        which = jnp.where(oy == ty, 2, jnp.where(oy < ty, 0, 1))
        bt[k * cells:(k + 1) * cells, :] = crecv[which, k].astype(F32).T.astype(BF16)
    ld_fine.wait()
    ld_lift.wait()

    def regrid_body(i, _):
        q = pl.multiple_of(i * pc, 128)
        g = jnp.dot(interp2[pl.ds(q, pc), :], bt[...], preferred_element_type=F32).astype(BF16)
        f = fine_v[pl.ds(q, pc), :].astype(F32) + jnp.dot(
            g, lift_v[...], preferred_element_type=F32)
        f = f.astype(BF16)
        field[pl.ds(q, pc), :] = f
        f = f.astype(F32)
        for r in range(cm):
            x_field[pl.ds(pl.multiple_of((i * cm + r + 2) * width + 16, 16), cols), :] = f[
                r * cols:(r + 1) * cols]
        return 0
    lax.fori_loop(0, px // pc, regrid_body, 0)

    h_field = rim_send(1, x_field, field)
    rim_take(1, x_field, h_field)
    widen(x_field, a_field)

    def pre_body(i, _):
        pre = conv_ext(a_field, wa_v, i * ce, ce)
        sig = 1.0 / (1.0 + jnp.exp(-pre))
        act = pre * sig
        bp = back_act[pl.ds(pl.multiple_of(i * (ce * ext), 16), ce * ext), :] * (
            sig * (1.0 + pre * (1.0 - sig)))
        for x, v in ((x_act, act), (x_bp, bp)):
            for r in range(ce):
                base = pl.multiple_of((i * ce + r + 1) * width, 16)
                o = r * ext
                x[pl.ds(base + 16, cols), :] = v[o:o + cols]
                x[pl.ds(base + 16 + cols, 8), :] = jnp.where(in_y[1], v[o + cols:o + cols + 8], 0.0)
                x[pl.ds(base + 8, 8), :] = jnp.where(in_y[0], v[o + cols + 8:o + ext], 0.0)
        return 0
    lax.fori_loop(0, (rows + 2) // ce, pre_body, 0)

    for inside, r in ((in_x[0], 1), (in_x[1], rows + 2)):
        @pl.when(jnp.logical_not(inside))
        def _():
            for x in (x_act, x_bp):
                x[r * width:(r + 1) * width, :] = jnp.zeros((width, chans), F32)

    widen_main(x_act, a_act)
    widen_main(x_bp, a_bp)

    def weight_grad(w, lhs, get):
        v = jnp.concatenate([get(d) for d in range(3)], axis=1)
        g = jnp.dot(lhs[...], v, preferred_element_type=F32)
        wsum[w] = g
        wsend[w] = g.astype(BF16)

    npx = px

    def first(w):
        n = 2 * (ny if w else nx)
        chunk = chans // n
        m = (cy if w else cx) * 2 + core
        cps = []
        for o in range(1, n):
            t = (m + o) % n
            peer = ((cx * ny + t // 2) if w else ((t // 2) * ny + cy)) * 2 + t % 2
            cps.append(remote(wsend.at[w, pl.ds(pl.multiple_of(t * chunk, 16), chunk), :],
                              w1.at[w, o - 1], wsnd.at[w, o - 1], wrcv.at[w, o - 1], peer, ty))
        return cps

    def second(w, cps):
        n = 2 * (ny if w else nx)
        chunk = chans // n
        m = (cy if w else cx) * 2 + core
        acc = wsum[w, pl.ds(pl.multiple_of(m * chunk, 16), chunk), :]
        for o, cp in enumerate(cps):
            cp.wait_recv()
            acc = acc + w1[w, o].astype(F32)
        n2 = nx if w else ny
        third = sz.taps // 3
        for s in range(n2):
            parts = [acc[s * span:(s + 1) * span, g * third:(g + 1) * third] for g in range(3)]
            if sz.pack > 3 * span:
                parts.append(jnp.zeros((sz.pack - 3 * span, third), F32))
            wst2[w, s] = jnp.concatenate(parts, axis=0).astype(BF16)
        mine = cx if w else cy
        nxt = []
        for o in range(1, n2):
            t = (mine + o) % n2
            peer = ((t * ny + cy) if w else (cx * ny + t)) * 2 + core
            nxt.append(remote(wst2.at[w, t], w2.at[w, o - 1],
                              wsnd.at[w, 8 + o], wrcv.at[w, 8 + o], peer, ty))
        return nxt

    def last(w, cps):
        mine = cx if w else cy
        acc = wst2[w, mine].astype(F32)
        for o, cp in enumerate(cps):
            cp.wait_recv()
            acc = acc + w2[w, o].astype(F32)
        w3[w, ty] = acc
        nxt = []
        for o in range(1, gy):
            nxt.append(remote(w3.at[w, ty], w3.at[w, ty], wsnd.at[w, 12 + o], wrcv.at[w, 12 + o],
                              tx, (ty + o) % gy))
        return nxt

    def finish(w, cps, dst):
        for cp in cps:
            cp.wait_recv()
        acc = w3[w, 0]
        for z in range(1, gy):
            acc = acc + w3[w, z]
        for g in range(3):
            for u in range(3):
                dst[3 * g + u] = acc[g * span:(g + 1) * span, u * chans:(u + 1) * chans]

    weight_grad(1, cot_t, lambda d: a_act[d * cols:d * cols + npx, :])
    sb = first(1)

    def turn_bp(i, _):
        q = pl.multiple_of(i * pc, 128)
        bp_t[:, pl.ds(q, pc)] = lax.dot_general(
            perm_a, a_bp[pl.ds(pl.multiple_of(q + cols, cols), pc), chans:2 * chans], NT,
            preferred_element_type=F32).astype(BF16)
        return 0
    lax.fori_loop(0, px // pc, turn_bp, 0)
    weight_grad(0, bp_t, lambda d: a_field[d + 1:d + 1 + rows, 0:cols, :].reshape(npx, 3 * chans))
    sa = first(0)

    def coarse_body(i, acc):
        q = pl.multiple_of(i * pc, 128)
        bf = (cot_v[pl.ds(q, pc), :].astype(F32) + conv_main(a_bp, wat, i * cm, cm)).astype(BF16)
        br = lax.dot_general(lift_v[...], bf, NT, preferred_element_type=F32).astype(BF16)
        return acc + jnp.dot(br, interp2[pl.ds(q, pc), :], preferred_element_type=F32)
    bb = lax.fori_loop(0, px // pc, coarse_body, jnp.zeros((chans_in, listed * cells), F32))
    for k in range(listed):
        v = bb[:, k * cells:(k + 1) * cells]
        gsum[k] = v
        gsend[k] = v.astype(BF16)
    d1 = [remote(gsend, g1.at[1], gsnd.at[0], grcv.at[0], tx, down),
          remote(gsend, g1.at[0], gsnd.at[1], grcv.at[1], tx, up)]

    sb = second(1, sb)
    sa = second(0, sa)

    def out_body(i, _):
        q = pl.multiple_of(i * pc, 128)
        out_v[pl.ds(q, pc), :] = (field[pl.ds(q, pc), :].astype(F32)
                                  + conv_main(a_act, wb_v, i * cm, cm)).astype(BF16)
        return 0
    lax.fori_loop(0, px // pc, out_body, 0)
    st_out = local(out_v, out, 7)

    for cp in d1:
        cp.wait_recv()
    cand = [(ids[k], lambda k=k: gsum[k]) for k in range(listed)]
    for s in range(2):
        for k in range(listed):
            cand.append((lsm[s, k, 0], lambda s=s, k=k: g1[s, k].astype(F32)))

    def spread(dx, m):
        want = ((tx + dx) * gy + ty) * nb + m
        acc = jnp.zeros((chans_in, cells), F32)
        for i, get in cand:
            acc = acc + jnp.where(i == want, get(), 0.0)
        return acc

    d2 = []
    for s, dx, to in ((0, -1, left), (1, 1, right)):
        def body(m, _):
            g2send[s, m] = spread(dx, m).astype(BF16)
            return 0
        lax.fori_loop(0, nb, body, 0)
        d2.append(remote(g2send.at[s], g2.at[1 - s], gsnd.at[2 + s], grcv.at[2 + s], to, ty))

    def own(m, _):
        gacc[m] = spread(0, m)
        return 0
    lax.fori_loop(0, nb, own, 0)

    sb = last(1, sb)
    sa = last(0, sa)
    finish(1, sb, gb)
    finish(0, sa, ga)
    for cp in d2:
        cp.wait_recv()

    def total(m, _):
        gc[m] = gacc[m] + g2[0, m].astype(F32) + g2[1, m].astype(F32)
        return 0
    lax.fori_loop(0, nb, total, 0)
    st_out.wait()
    for cp in started:
        cp.wait_send()


def fused(sz, lists, coarse, interp, fine, lift, wa, wb, cot):
    rows, cols, chans, px, width, ext = sz.rows, sz.cols, sz.chans, sz.px, sz.width, sz.ext
    nb, ci, cells, listed = sz.blocks, sz.chans_in, sz.cells, sz.listed
    n1 = 2 * max(sz.nx, sz.ny) - 1
    n2 = max(sz.nx, sz.ny)
    chunk = chans // (2 * min(sz.nx, sz.ny))
    vm = pltpu.VMEM
    dma = pltpu.SemaphoreType.DMA
    anyspace = pl.BlockSpec(memory_space=pl.ANY)
    vspace = pl.BlockSpec(memory_space=pltpu.VMEM)
    x = vm(((rows + 4) * width, chans), F32)
    a_ext = vm((rows + 4, ext, 3 * chans), BF16)
    a_main = vm(((rows + 2) * cols, 3 * chans), BF16)
    scratch = [
        vm((3, nb, ci, cells), BF16), vm((8, 128), jnp.int32), vm((2, 8, 128), jnp.int32),
        pltpu.SMEM((2, 8, 128), jnp.int32), vm((2, listed, ci, cells), BF16),
        vm((3, listed, ci, cells), BF16),
        vm((px * listed, cells), BF16), vm((px * listed // 8, cells), F32),
        vm((px, listed * cells), BF16), vm((px, chans), BF16), vm((ci, chans), BF16),
        vm((9 * chans, chans), BF16), vm((9 * chans, chans), BF16),
        vm((9 * chans, chans), BF16), vm((9 * chans, chans), BF16),
        vm((px, chans), BF16), vm((listed * cells, ci), BF16),
        x, x, x, x, a_ext, a_ext, a_main, a_main,
        vm(((rows + 2) * ext, chans), F32), vm((px, chans), BF16), vm((px, chans), BF16),
        vm((chans, px), BF16), vm((chans, px), BF16),
        vm((2, 2, 2 * rows, chans), BF16), vm((2, 4, 16, chans), BF16),
        vm((2, 2, 2 * cols, chans), BF16), vm((2, 2, 2 * rows, chans), BF16),
        vm((2, 4, 16, chans), BF16),
        vm((2, chans, 9 * chans), F32), vm((2, chans, 9 * chans), BF16),
        vm((2, n1, chunk, 9 * chans), BF16),
        vm((2, n2, sz.pack, 3 * chans), BF16), vm((2, n2 - 1, sz.pack, 3 * chans), BF16),
        vm((2, sz.gy, sz.pack, 3 * chans), F32),
        vm((listed, ci, cells), F32), vm((listed, ci, cells), BF16), vm((2, listed, ci, cells), BF16),
        vm((2, nb, ci, cells), BF16), vm((2, nb, ci, cells), BF16), vm((nb, ci, cells), F32),
        dma((8,)), dma, dma((6,)), dma((6,)), dma((2, 8)), dma((2, 8)),
        dma((2, 16)), dma((2, 16)), dma((4,)), dma((4,)),
    ]
    flops = 2 * px * (6 * 9 * chans * chans + 2 * listed * cells * ci + 2 * ci * chans)
    return pl.pallas_call(
        functools.partial(kernel, sz),
        out_shape=(
            jax.ShapeDtypeStruct((px, chans), BF16),
            jax.ShapeDtypeStruct((9, sz.span, chans), F32),
            jax.ShapeDtypeStruct((9, sz.span, chans), F32),
            jax.ShapeDtypeStruct((nb, ci, cells), F32),
        ),
        in_specs=[pl.BlockSpec(memory_space=pltpu.SMEM)] + [anyspace] * 7,
        out_specs=(anyspace, vspace, vspace, vspace),
        scratch_shapes=scratch,
        compiler_params=pltpu.CompilerParams(
            collective_id=0, has_side_effects=True, vmem_limit_bytes=56 * MIB),
        cost_estimate=pl.CostEstimate(flops=flops, bytes_accessed=5 * MIB, transcendentals=px * chans),
    )(lists, coarse, interp, fine, lift, wa, wb, cot)


def on_device(nx, ny, coarse, lists, interp, fine_own, lift, conv_a, conv_b, cotangent):
    rows, cols, chans = fine_own.shape
    listed, cells = interp.shape[2:]
    blocks, chans_in = coarse.shape[2:4]
    sz = Sizes(lax.axis_size("gx"), lax.axis_size("gy"), nx, ny, rows, cols, chans, chans_in,
               cells, listed, blocks)
    output, ga, gb, gc = fused(
        sz,
        lists.reshape(1, listed),
        coarse.reshape(blocks, chans_in, cells),
        interp.reshape(rows * cols * listed, cells),
        fine_own.reshape(rows * cols, chans),
        lift,
        conv_a.reshape(9 * chans, chans),
        conv_b.reshape(9 * chans, chans),
        cotangent.reshape(rows * cols, chans),
    )
    return (
        output.reshape(rows, cols, chans),
        jnp.transpose(ga, (0, 2, 1)),
        jnp.transpose(gb, (0, 2, 1)),
        gc.reshape(1, 1, blocks, chans_in, cells),
    )


def solution(mesh):
    side = {32: 4, 8: 2}[mesh.shape["gx"]]
    placed = (
        P("gx", "gy", None, None, None),
        P("gx", "gy", None),
        P("gx", "gy", None, None),
        P("gx", "gy", None),
        P(),
        P(),
        P(),
        P("gx", "gy", None),
    )
    return jax.shard_map(
        functools.partial(on_device, side, side),
        mesh=mesh,
        in_specs=placed,
        out_specs=(
            P("gx", "gy", None),
            P(None, None, "gx"),
            P(None, None, "gx"),
            P("gx", "gy", None, None, None),
        ),
        check_vma=False,
    )
```

```python
import functools

import jax
import jax.numpy as jnp
from jax import lax
from jax.experimental import pallas as pl
from jax.experimental.pallas import tpu as pltpu
from jax.sharding import PartitionSpec as P

MESH = pl.DeviceIdType.MESH
F32 = jnp.float32
BF16 = jnp.bfloat16
MIB = 1024 * 1024
NT = (((1,), (1,)), ((), ()))
AROUND = ((-1, 0), (1, 0), (0, -1), (0, 1), (-1, -1), (1, 1), (-1, 1), (1, -1))


class Sizes:
    def __init__(self, gx, gy, nx, ny, rows, cols, chans, chans_in, cells, listed, blocks):
        self.gx, self.gy, self.nx, self.ny = gx, gy, nx, ny
        self.rows, self.cols = rows, cols
        self.chans, self.chans_in, self.cells = chans, chans_in, cells
        self.listed, self.blocks = listed, blocks
        self.px = rows * cols
        self.width = cols + 32
        self.span = chans // gx
        self.pack = -(-3 * self.span // 16) * 16
        self.plane = nx * ny


def kernel(
    sz,
    lists, coarse, interp, fine, lift, wa, wb, cot,
    out, ga, gb, gc,
    call, lvec, lrecv, lsm, picked, crecv,
    raw, rawf, interp2, fine_v, lift_v, wa_v, wb_v, wat, wbt, w2_a, w2_b, w2_at, w2_bt, cot_v, bt,
    x_cot, x_field, x_act, x_bp, a_cot, a_field, s_cot, s_field, a_act, a_bp,
    ba_main, ba_strip, field, out_v, cot_t, bp_t,
    hs_cols, hs_corner, hr_rows, hr_cols, hr_corner,
    wsum, wsend, w1, wst2, w2, w3,
    gsum, gsend, g1,
    local_sem, lsem, csend, crcv, hsend, hrcv, wsnd, wrcv, gsnd, grcv,
):
    tx = lax.axis_index("gx")
    ty = lax.axis_index("gy")
    gx, gy, nx, ny = sz.gx, sz.gy, sz.nx, sz.ny
    rows, cols, chans, width, px = sz.rows, sz.cols, sz.chans, sz.width, sz.px
    listed, cells, chans_in, nb, span = sz.listed, sz.cells, sz.chans_in, sz.blocks, sz.span
    core = tx % 2
    mine = tx // 2
    around = [((tx + dx + gx) % gx, (ty + dy + gy) % gy) for dx, dy in AROUND]
    started = []

    def remote(src, dst, ssem, rsem, px_, py_):
        copy = pltpu.make_async_remote_copy(
            src_ref=src, dst_ref=dst, send_sem=ssem, recv_sem=rsem,
            device_id=(px_, py_), device_id_type=MESH,
        )
        copy.start()
        started.append(copy)
        return copy

    def local(src, dst, i):
        copy = pltpu.make_async_copy(src, dst, local_sem.at[i])
        copy.start()
        return copy

    ld_coarse = local(coarse, call.at[1], 0)
    ld_cot = local(cot, cot_v, 1)
    ld_wb = local(wb, wb_v, 3)
    ld_raw = local(interp, raw, 2)
    ld_wa = local(wa, wa_v, 4)
    ld_fine = local(fine, fine_v, 5)
    ld_lift = local(lift, lift_v, 6)

    peers = list(around)
    for o in range(2, gy - 1):
        peers.append((tx, (ty + o) % gy))
    for o in range(1, sz.plane):
        peers.append((((mine + o) % sz.plane) * 2 + core, ty))
    barrier = pltpu.get_barrier_semaphore()
    for p in peers:
        pl.semaphore_signal(barrier, inc=1, device_id=p, device_id_type=MESH)
    rowi = lax.broadcasted_iota(jnp.int32, (8, 128), 0)
    vec = jnp.zeros((8, 128), jnp.int32)
    for k in range(listed):
        vec = jnp.where(rowi == k, lists[0, k], vec)
    lvec[...] = vec
    ld_coarse.wait()
    ld_cot.wait()

    def fill(x, src):
        for r in range(rows):
            x[(r + 2) * width + 16:(r + 2) * width + 16 + cols, :] = src[
                r * cols:(r + 1) * cols].astype(F32)

    fill(x_cot, cot_v)
    pl.semaphore_wait(barrier, len(peers))

    c1 = [remote(call.at[1], call.at[2], csend.at[0], crcv.at[0], *around[0]),
          remote(call.at[1], call.at[0], csend.at[1], crcv.at[1], *around[1])]
    l1 = [None] * 8
    for i in (2, 3, 0, 1, 4, 5, 6, 7):
        l1[i] = remote(lvec, lrecv.at[i ^ 1], csend.at[4 + i], crcv.at[4 + i], *around[i])

    def rim_send(e, x, main):
        cps = []
        n2 = 2 * cols
        cps.append(remote(main.at[pl.ds(0, n2), :], hr_rows.at[e, 1],
                          hsend.at[e, 0], hrcv.at[e, 0], *around[0]))
        cps.append(remote(main.at[pl.ds(px - n2, n2), :], hr_rows.at[e, 0],
                          hsend.at[e, 1], hrcv.at[e, 1], *around[1]))
        for s, c0 in ((0, 0), (1, cols - 2)):
            for j in range(2):
                hs_cols[e, s, j * rows:(j + 1) * rows, :] = x[
                    pl.ds(2 * width + 16 + c0 + j, rows, stride=width), :].astype(BF16)
        cps.append(remote(hs_cols.at[e, 0], hr_cols.at[e, 1],
                          hsend.at[e, 2], hrcv.at[e, 2], *around[2]))
        cps.append(remote(hs_cols.at[e, 1], hr_cols.at[e, 0],
                          hsend.at[e, 3], hrcv.at[e, 3], *around[3]))
        q = 0
        for r0, i0 in ((0, (4, 6)), (rows - 2, (7, 5))):
            for c0, i in ((0, i0[0]), (cols - 2, i0[1])):
                parts = [x[(2 + r0 + i_) * width + 16 + c0:(2 + r0 + i_) * width + 18 + c0, :]
                         for i_ in range(2)]
                parts.append(jnp.zeros((12, chans), F32))
                hs_corner[e, q] = jnp.concatenate(parts, axis=0).astype(BF16)
                cps.append(remote(hs_corner.at[e, q], hr_corner.at[e, 3 - q],
                                  hsend.at[e, 4 + q], hrcv.at[e, 4 + q], *around[i]))
                q += 1
        return cps

    in_x = (tx > 0, tx < gx - 1)
    in_y = (ty > 0, ty < gy - 1)

    def rim_take(e, x, cps):
        for cp in cps:
            cp.wait_recv()
        for s, r0 in ((0, 0), (1, rows + 2)):
            v = jnp.where(in_x[s], hr_rows[e, s].astype(F32), 0.0)
            for i in range(2):
                x[(r0 + i) * width + 16:(r0 + i) * width + 16 + cols, :] = v[i * cols:(i + 1) * cols]
        for s, c0 in ((0, 14), (1, 16 + cols)):
            v = jnp.where(in_y[s], hr_cols[e, s].astype(F32), 0.0)
            for j in range(2):
                x[pl.ds(2 * width + c0 + j, rows, stride=width), :] = v[j * rows:(j + 1) * rows]
        q = 0
        for sr, r0 in ((0, 0), (1, rows + 2)):
            for sc, c0 in ((0, 14), (1, 16 + cols)):
                v = jnp.where(jnp.logical_and(in_x[sr], in_y[sc]),
                              hr_corner[e, q].astype(F32), 0.0)
                for i in range(2):
                    x[(r0 + i) * width + c0:(r0 + i) * width + c0 + 2, :] = v[2 * i:2 * i + 2]
                q += 1

    def widen(x, a, first, last, shift):
        for r in range(first, last):
            for dj in range(3):
                c = r * width + 15 + dj
                a[(r - shift) * cols:(r - shift + 1) * cols, dj * chans:(dj + 1) * chans] = x[
                    c:c + cols, :].astype(BF16)

    def widen_edge(x, a, first, last):
        for r in range(first, last):
            c = r * width + 15
            a[r * cols:r * cols + 16, 0:chans] = x[c:c + 16, :].astype(BF16)
            c = r * width + 17 + cols - 16
            a[(r + 1) * cols - 16:(r + 1) * cols, 2 * chans:3 * chans] = x[c:c + 16, :].astype(BF16)

    def widen_strip(x, s):
        for r in range(rows + 4):
            for dj in range(3):
                c = r * width + 15 + dj
                v = jnp.concatenate(
                    [x[c + cols - 4:c + cols + 4, :], x[c - 4:c + 4, :]], axis=0)
                s[r * 16:(r + 1) * 16, dj * chans:(dj + 1) * chans] = v.astype(BF16)

    def conv_pairs(a, w2x, first, pairs):
        v = jnp.concatenate([
            jnp.concatenate([a[(first + 2 * p + d) * cols:(first + 2 * p + d + 1) * cols, :]
                             for p in range(pairs)], axis=0) for d in range(4)], axis=1)
        res = jnp.dot(v, w2x[...], preferred_element_type=F32)
        return [(first + 2 * p + s, res[p * cols:(p + 1) * cols, s * chans:(s + 1) * chans])
                for p in range(pairs) for s in range(2)]

    def conv_strip(s, w):
        v = jnp.concatenate([s[d * 16:(d + rows + 2) * 16, :] for d in range(3)], axis=1)
        return jnp.dot(v, w[...], preferred_element_type=F32)

    h_cot = rim_send(0, x_cot, cot_v)

    third = 3 * chans
    ld_wb.wait()
    ld_wa.wait()
    for src, flip, two, two_flip in ((wb_v, wbt, w2_b, w2_bt), (wa_v, wat, w2_a, w2_at)):
        for t in range(9):
            flip[t * chans:(t + 1) * chans, :] = src[
                (8 - t) * chans:(9 - t) * chans, :].astype(F32).T.astype(BF16)
        for one, both in ((src, two), (flip, two_flip)):
            both[0:3 * third, 0:chans] = one[...]
            both[third:4 * third, chans:2 * chans] = one[...]
            both[3 * third:4 * third, 0:chans] = jnp.zeros((third, chans), BF16)
            both[0:third, chans:2 * chans] = jnp.zeros((third, chans), BF16)

    ld_raw.wait()
    step = px // 8

    def relay(i, _):
        rawf[...] = raw[pl.ds(pl.multiple_of(i * step * listed, 16), step * listed), :].astype(F32)
        for k in range(listed):
            interp2[pl.ds(pl.multiple_of(i * step, 16), step), k * cells:(k + 1) * cells] = rawf[
                pl.ds(k, step, stride=listed), :].astype(BF16)
        return 0
    lax.fori_loop(0, 8, relay, 0)

    ri = lax.broadcasted_iota(jnp.int32, (chans, chans), 0)
    ci = lax.broadcasted_iota(jnp.int32, (chans, chans), 1)
    half = chans // 2
    rest = ri % half
    perm = jnp.where(
        ci == (rest // span) * 2 * span + (ri // half) * span + rest % span, 1.0, 0.0).astype(BF16)
    cot_t[...] = lax.dot_general(perm, cot_v[...], NT, preferred_element_type=F32).astype(BF16)

    for cp in c1 + l1[2:4]:
        cp.wait_recv()
    ld_l = pltpu.make_async_copy(lrecv.at[pl.ds(2, 2)], lsm.at[pl.ds(2, 2)], lsem.at[0])
    ld_l.start()
    ld_l.wait()

    def clip(v):
        return jnp.minimum(jnp.maximum(v, 0), 2)

    c2 = []
    for s in (2, 3):
        for k in range(listed):
            i = lsm[s, k, 0]
            picked[s - 2, k] = call[clip(i // (nb * gy) - tx + 1), i % nb]
        c2.append(remote(picked.at[s - 2], crecv.at[3 - s], csend.at[s], crcv.at[s], *around[s]))
    ids = [lists[0, k] for k in range(listed)]
    for k in range(listed):
        i = ids[k]
        crecv[2, k] = call[clip(i // (nb * gy) - tx + 1), i % nb]

    rim_take(0, x_cot, h_cot)
    widen(x_cot, a_cot, 0, rows + 4, 0)
    widen_strip(x_cot, s_cot)
    for r, v in conv_pairs(a_cot, w2_bt, 0, (rows + 2) // 2):
        ba_main[r * cols:(r + 1) * cols, :] = v
    ba_strip[...] = conv_strip(s_cot, wbt)

    for cp in c2:
        cp.wait_recv()
    for k in range(listed):
        oy = (ids[k] // nb) % gy
        which = jnp.where(oy == ty, 2, jnp.where(oy < ty, 0, 1))
        bt[k * cells:(k + 1) * cells, :] = crecv[which, k].astype(F32).T.astype(BF16)
    ld_fine.wait()
    ld_lift.wait()
    g = jnp.dot(interp2[...], bt[...], preferred_element_type=F32).astype(BF16)
    f = fine_v[...].astype(F32) + jnp.dot(g, lift_v[...], preferred_element_type=F32)
    f = f.astype(BF16)
    field[...] = f
    fill(x_field, f)

    h_field = rim_send(1, x_field, field)
    widen(x_field, a_field, 2, rows + 2, 0)

    def point(pre, back):
        sig = 1.0 / (1.0 + jnp.exp(-pre))
        return pre * sig, back * (sig * (1.0 + pre * (1.0 - sig)))

    def keep(r, pre):
        act, bp = point(pre, ba_main[r * cols:(r + 1) * cols, :])
        c = (r + 1) * width + 16
        x_act[c:c + cols, :] = act
        x_bp[c:c + cols, :] = bp

    for r, pre in conv_pairs(a_field, w2_a, 2, (rows - 2) // 2):
        keep(r, pre)

    rim_take(1, x_field, h_field)
    widen(x_field, a_field, 0, 2, 0)
    widen(x_field, a_field, rows + 2, rows + 4, 0)
    widen_edge(x_field, a_field, 2, rows + 2)
    widen_strip(x_field, s_field)
    for r0 in (0, rows):
        for r, pre in conv_pairs(a_field, w2_a, r0, 1):
            keep(r, pre)
    pre = conv_strip(s_field, wa_v)
    act, bp = point(pre, ba_strip[...])
    inside = lax.broadcasted_iota(jnp.int32, (8, chans), 0)
    far = jnp.logical_or(inside < 4, in_y[1])
    near = jnp.logical_or(inside >= 4, in_y[0])
    for x, v in ((x_act, act), (x_bp, bp)):
        for r in range(rows + 2):
            c = (r + 1) * width + 16
            x[c + cols - 4:c + cols + 4, :] = jnp.where(far, v[r * 16:r * 16 + 8], 0.0)
            x[c - 4:c + 4, :] = jnp.where(near, v[r * 16 + 8:r * 16 + 16], 0.0)

    for ok, r in ((in_x[0], 1), (in_x[1], rows + 2)):
        @pl.when(jnp.logical_not(ok))
        def _():
            for x in (x_act, x_bp):
                x[r * width:(r + 1) * width, :] = jnp.zeros((width, chans), F32)

    def weight_grad(w, lhs, a, first):
        v = jnp.concatenate([a[(first + d) * cols:(first + d) * cols + px, :] for d in range(3)],
                            axis=1)
        g = jnp.dot(lhs, v, preferred_element_type=F32)
        wsum[w] = g
        wsend[w] = g.astype(BF16)

    def first(w):
        other = 1 - core
        return remote(wsend.at[w, pl.ds(pl.multiple_of(other * half, 16), half), :],
                      w1.at[w], wsnd.at[w, 0], wrcv.at[w, 0], mine * 2 + other, ty)

    def second(w, cp):
        own = wsum[w, pl.ds(pl.multiple_of(core * half, 16), half), :]
        cp.wait_recv()
        acc = own + w1[w].astype(F32)
        for s in range(sz.plane):
            parts = [acc[s * span:(s + 1) * span, g * third:(g + 1) * third] for g in range(3)]
            if sz.pack > 3 * span:
                parts.append(jnp.zeros((sz.pack - 3 * span, third), F32))
            wst2[w, s] = jnp.concatenate(parts, axis=0).astype(BF16)
        nxt = []
        for o in range(1, sz.plane):
            t = (mine + o) % sz.plane
            nxt.append(remote(wst2.at[w, t], w2.at[w, o - 1],
                              wsnd.at[w, o], wrcv.at[w, o], t * 2 + core, ty))
        return nxt

    def last(w, cps):
        acc = wst2[w, mine].astype(F32)
        for o, cp in enumerate(cps):
            cp.wait_recv()
            acc = acc + w2[w, o].astype(F32)
        w3[w, ty] = acc
        nxt = []
        for o in range(1, gy):
            j = sz.plane + o
            nxt.append(remote(w3.at[w, ty], w3.at[w, ty], wsnd.at[w, j], wrcv.at[w, j],
                              tx, (ty + o) % gy))
        return nxt

    def finish(w, cps, dst):
        for cp in cps:
            cp.wait_recv()
        acc = w3[w, 0]
        for z in range(1, gy):
            acc = acc + w3[w, z]
        for g in range(3):
            for u in range(3):
                dst[3 * g + u] = acc[g * span:(g + 1) * span, u * chans:(u + 1) * chans]

    widen(x_act, a_act, 1, rows + 3, 1)
    weight_grad(1, cot_t[...], a_act, 0)
    sb = first(1)
    widen(x_bp, a_bp, 1, rows + 3, 1)
    bp_t[...] = lax.dot_general(
        perm, a_bp[cols:cols + px, chans:2 * chans], NT, preferred_element_type=F32).astype(BF16)
    weight_grad(0, bp_t[...], a_field, 1)
    sa = first(0)
    sb = second(1, sb)

    bf = [(cot_v[r * cols:(r + 1) * cols, :].astype(F32) + v).astype(BF16)
          for r, v in conv_pairs(a_bp, w2_at, 0, rows // 2)]
    br = lax.dot_general(lift_v[...], jnp.concatenate(bf, axis=0), NT,
                         preferred_element_type=F32).astype(BF16)
    sa = second(0, sa)
    bb = jnp.dot(br, interp2[...], preferred_element_type=F32)
    for k in range(listed):
        v = bb[:, k * cells:(k + 1) * cells]
        gsum[k] = v
        gsend[k] = v.astype(BF16)
    d1 = [remote(gsend, g1.at[i ^ 1], gsnd.at[i], grcv.at[i], *around[i]) for i in range(8)]

    for r, v in conv_pairs(a_act, w2_b, 0, rows // 2):
        q = slice(r * cols, (r + 1) * cols)
        out_v[q, :] = (field[q, :].astype(F32) + v).astype(BF16)
    st_out = local(out_v, out, 7)

    sb = last(1, sb)
    sa = last(0, sa)
    for i in (0, 1, 4, 5, 6, 7):
        l1[i].wait_recv()
    ld_m = [pltpu.make_async_copy(lrecv.at[pl.ds(i, n)], lsm.at[pl.ds(i, n)], lsem.at[j])
            for j, (i, n) in ((1, (0, 2)), (2, (4, 4)))]
    for cp in ld_m:
        cp.start()
    for cp in ld_m:
        cp.wait()
    for cp in d1:
        cp.wait_recv()
    cand = [(ids[k], lambda k=k: gsum[k]) for k in range(listed)]
    for s in range(8):
        for k in range(listed):
            cand.append((lsm[s, k, 0], lambda s=s, k=k: g1[s, k].astype(F32)))
    base = (tx * gy + ty) * nb

    def total(m, _):
        acc = jnp.zeros((chans_in, cells), F32)
        for i, get in cand:
            acc = acc + jnp.where(i == base + m, get(), 0.0)
        gc[m] = acc
        return 0
    lax.fori_loop(0, nb, total, 0)
    finish(1, sb, gb)
    finish(0, sa, ga)
    st_out.wait()
    for cp in started:
        cp.wait_send()


def hand_out(*refs):
    count = (len(refs) - 1) // 2
    sems = refs[-1]
    copies = [pltpu.make_async_copy(refs[i], refs[count + i], sems.at[i]) for i in range(count)]
    for cp in copies:
        cp.start()
    for cp in copies:
        cp.wait()


def fused(sz, lists, coarse, interp, fine, lift, wa, wb, cot):
    rows, cols, chans, px, width = sz.rows, sz.cols, sz.chans, sz.px, sz.width
    nb, ci, cells, listed = sz.blocks, sz.chans_in, sz.cells, sz.listed
    vm = pltpu.VMEM
    dma = pltpu.SemaphoreType.DMA
    anyspace = pl.BlockSpec(memory_space=pl.ANY)
    vspace = pl.BlockSpec(memory_space=pltpu.VMEM)
    x = vm(((rows + 4) * width, chans), F32)
    a_ext = vm(((rows + 4) * cols, 3 * chans), BF16)
    strip = vm(((rows + 4) * 16, 3 * chans), BF16)
    a_main = vm(((rows + 2) * cols, 3 * chans), BF16)
    w = vm((9 * chans, chans), BF16)
    w2 = vm((12 * chans, 2 * chans), BF16)
    scratch = [
        vm((3, nb, ci, cells), BF16), vm((8, 128), jnp.int32), vm((8, 8, 128), jnp.int32),
        pltpu.SMEM((8, 8, 128), jnp.int32), vm((2, listed, ci, cells), BF16),
        vm((3, listed, ci, cells), BF16),
        vm((px * listed, cells), BF16), vm((px * listed // 8, cells), F32),
        vm((px, listed * cells), BF16), vm((px, chans), BF16), vm((ci, chans), BF16),
        w, w, w, w, w2, w2, w2, w2,
        vm((px, chans), BF16), vm((listed * cells, ci), BF16),
        x, x, x, x, a_ext, a_ext, strip, strip, a_main, a_main,
        vm(((rows + 2) * cols, chans), F32), vm(((rows + 2) * 16, chans), F32),
        vm((px, chans), BF16), vm((px, chans), BF16),
        vm((chans, px), BF16), vm((chans, px), BF16),
        vm((2, 2, 2 * rows, chans), BF16), vm((2, 4, 16, chans), BF16),
        vm((2, 2, 2 * cols, chans), BF16), vm((2, 2, 2 * rows, chans), BF16),
        vm((2, 4, 16, chans), BF16),
        vm((2, chans, 9 * chans), F32), vm((2, chans, 9 * chans), BF16),
        vm((2, chans // 2, 9 * chans), BF16),
        vm((2, sz.plane, sz.pack, 3 * chans), BF16),
        vm((2, sz.plane - 1, sz.pack, 3 * chans), BF16),
        vm((2, sz.gy, sz.pack, 3 * chans), F32),
        vm((listed, ci, cells), F32), vm((listed, ci, cells), BF16),
        vm((8, listed, ci, cells), BF16),
        dma((8,)), dma((3,)), dma((12,)), dma((12,)), dma((2, 8)), dma((2, 8)),
        dma((2, sz.plane + sz.gy)), dma((2, sz.plane + sz.gy)), dma((8,)), dma((8,)),
    ]
    flops = 2 * px * (6 * 9 * chans * chans + 2 * listed * cells * ci + 2 * ci * chans)
    shapes = (
        jax.ShapeDtypeStruct((px, chans), BF16),
        jax.ShapeDtypeStruct((9, sz.span, chans), F32),
        jax.ShapeDtypeStruct((9, sz.span, chans), F32),
        jax.ShapeDtypeStruct((nb, ci, cells), F32),
    )
    results = pl.pallas_call(
        functools.partial(kernel, sz),
        out_shape=shapes,
        in_specs=[pl.BlockSpec(memory_space=pltpu.SMEM)] + [anyspace] * 7,
        out_specs=(anyspace, vspace, vspace, vspace),
        scratch_shapes=scratch,
        compiler_params=pltpu.CompilerParams(
            collective_id=0, has_side_effects=True, vmem_limit_bytes=56 * MIB),
        cost_estimate=pl.CostEstimate(flops=flops, bytes_accessed=5 * MIB, transcendentals=px * chans),
    )(lists, coarse, interp, fine, lift, wa, wb, cot)
    return pl.pallas_call(
        hand_out,
        out_shape=shapes,
        in_specs=[vspace] * 4,
        out_specs=(anyspace,) * 4,
        scratch_shapes=[dma((4,))],
    )(*results)


def on_device(nx, ny, coarse, lists, interp, fine_own, lift, conv_a, conv_b, cotangent):
    rows, cols, chans = fine_own.shape
    listed, cells = interp.shape[2:]
    blocks, chans_in = coarse.shape[2:4]
    sz = Sizes(lax.axis_size("gx"), lax.axis_size("gy"), nx, ny, rows, cols, chans, chans_in,
               cells, listed, blocks)
    output, ga, gb, gc = fused(
        sz,
        lists.reshape(1, listed),
        coarse.reshape(blocks, chans_in, cells),
        interp.reshape(rows * cols * listed, cells),
        fine_own.reshape(rows * cols, chans),
        lift,
        conv_a.reshape(9 * chans, chans),
        conv_b.reshape(9 * chans, chans),
        cotangent.reshape(rows * cols, chans),
    )
    return (
        output.reshape(rows, cols, chans),
        jnp.transpose(ga, (0, 2, 1)),
        jnp.transpose(gb, (0, 2, 1)),
        gc.reshape(1, 1, blocks, chans_in, cells),
    )


def solution(mesh):
    side = {32: 4, 8: 2}[mesh.shape["gx"]]
    placed = (
        P("gx", "gy", None, None, None),
        P("gx", "gy", None),
        P("gx", "gy", None, None),
        P("gx", "gy", None),
        P(),
        P(),
        P(),
        P("gx", "gy", None),
    )
    return jax.shard_map(
        functools.partial(on_device, side, side),
        mesh=mesh,
        in_specs=placed,
        out_specs=(
            P("gx", "gy", None),
            P(None, None, "gx"),
            P(None, None, "gx"),
            P("gx", "gy", None, None, None),
        ),
        check_vma=False,
    )
```

```python
import functools

import jax
import jax.numpy as jnp
from jax import lax
from jax.experimental import pallas as pl
from jax.experimental.pallas import tpu as pltpu
from jax.sharding import PartitionSpec as P

MESH = pl.DeviceIdType.MESH
F32 = jnp.float32
BF16 = jnp.bfloat16
MIB = 1024 * 1024
PARTS = 2
NT = (((1,), (1,)), ((), ()))
AROUND = ((-1, 0), (1, 0), (0, -1), (0, 1), (-1, -1), (1, 1), (-1, 1), (1, -1))


class Sizes:
    def __init__(self, gx, gy, nx, ny, rows, cols, chans, chans_in, cells, listed, blocks):
        self.gx, self.gy, self.nx, self.ny = gx, gy, nx, ny
        self.rows, self.cols = rows, cols
        self.chans, self.chans_in, self.cells = chans, chans_in, cells
        self.listed, self.blocks = listed, blocks
        self.px = rows * cols
        self.width = cols + 32
        self.span = chans // gx
        self.pack = -(-3 * self.span // 16) * 16
        self.plane = nx * ny


def kernel(
    sz,
    lists, coarse, interp, fine, lift, wa, wb, cot,
    out, ga, gb, gc,
    call0, call1, lvec, lrecv, lsm, picked, crecv,
    raw, rawf, interp2, fine_v, lift_v, wa_v, wb_v, wat, wbt, w2_a, w2_b, w2_at, w2_bt, cot_v, bt,
    x_cot, x_field, x_act, x_bp, a_cot, a_field, s_cot, s_field, a_act, a_bp,
    side_act, side_field, ba_main, ba_strip, field, out_v, cot_t, cot_r,
    hs_cols, hs_corner, hr_rows, hr_cols, hr_corner,
    wsum, wsend, w1, wst2, w2, w3,
    gsum, gsend, g1,
    local_sem, lsem, csend, crcv, c1s, c1r, c2s, c2r, hsend, hrcv, wsnd, wrcv, gsnd, grcv,
):
    tx = lax.axis_index("gx")
    ty = lax.axis_index("gy")
    gx, gy, nx, ny = sz.gx, sz.gy, sz.nx, sz.ny
    rows, cols, chans, width, px = sz.rows, sz.cols, sz.chans, sz.width, sz.px
    listed, cells, chans_in, nb, span = sz.listed, sz.cells, sz.chans_in, sz.blocks, sz.span
    core = tx % 2
    mine = tx // 2
    around = [((tx + dx + gx) % gx, (ty + dy + gy) % gy) for dx, dy in AROUND]
    started = []

    def remote(src, dst, ssem, rsem, px_, py_):
        copy = pltpu.make_async_remote_copy(
            src_ref=src, dst_ref=dst, send_sem=ssem, recv_sem=rsem,
            device_id=(px_, py_), device_id_type=MESH,
        )
        copy.start()
        started.append(copy)
        return copy

    def local(src, dst, i):
        copy = pltpu.make_async_copy(src, dst, local_sem.at[i])
        copy.start()
        return copy

    calls = (call0, call1)
    part = chans_in // PARTS
    cuts = [pl.ds(h * part, part) for h in range(PARTS)]
    ld_coarse = [local(coarse.at[:, cut], calls[h].at[1], 7 * h) for h, cut in enumerate(cuts)]
    ld_cot = local(cot, cot_v, 1)
    ld_wb = local(wb, wb_v, 3)
    ld_raw = local(interp, raw, 2)
    ld_wa = local(wa, wa_v, 4)
    ld_fine = local(fine, fine_v, 5)
    ld_lift = local(lift, lift_v, 6)

    peers = list(around)
    for o in range(2, gy - 1):
        peers.append((tx, (ty + o) % gy))
    for o in range(1, sz.plane):
        peers.append((((mine + o) % sz.plane) * 2 + core, ty))
    barrier = pltpu.get_barrier_semaphore()
    for p in peers:
        pl.semaphore_signal(barrier, inc=1, device_id=p, device_id_type=MESH)
    rowi = lax.broadcasted_iota(jnp.int32, (8, 128), 0)
    vec = jnp.zeros((8, 128), jnp.int32)
    for k in range(listed):
        vec = jnp.where(rowi == k, lists[0, k], vec)
    lvec[...] = vec

    def fill(x, src):
        for r in range(rows):
            x[(r + 2) * width + 16:(r + 2) * width + 16 + cols, :] = src[
                r * cols:(r + 1) * cols].astype(F32)

    pl.semaphore_wait(barrier, len(peers))

    l1 = {}

    def tell(i):
        l1[i] = remote(lvec, lrecv.at[i ^ 1], csend.at[4 + i], crcv.at[4 + i], *around[i])

    tell(2)
    tell(3)
    c1 = [[remote(coarse.at[:, cut], calls[h].at[2 - 2 * i], c1s.at[h, i], c1r.at[h, i], *around[i])
           for i in range(2)] for h, cut in enumerate(cuts)]

    def rim_rows(e, x, main):
        n2 = 2 * cols
        cps = [remote(main.at[pl.ds(0, n2), :], hr_rows.at[e, 1],
                      hsend.at[e, 0], hrcv.at[e, 0], *around[0]),
               remote(main.at[pl.ds(px - n2, n2), :], hr_rows.at[e, 0],
                      hsend.at[e, 1], hrcv.at[e, 1], *around[1])]
        q = 0
        for r0, i0 in ((0, (4, 6)), (rows - 2, (7, 5))):
            for c0, i in ((0, i0[0]), (cols - 2, i0[1])):
                parts = [x[(2 + r0 + k) * width + 16 + c0:(2 + r0 + k) * width + 18 + c0, :]
                         for k in range(2)]
                parts.append(jnp.zeros((12, chans), F32))
                hs_corner[e, q] = jnp.concatenate(parts, axis=0).astype(BF16)
                cps.append(remote(hs_corner.at[e, q], hr_corner.at[e, 3 - q],
                                  hsend.at[e, 4 + q], hrcv.at[e, 4 + q], *around[i]))
                q += 1
        return cps

    def rim_cols(e, x):
        for s, c0 in ((0, 0), (1, cols - 2)):
            for j in range(2):
                hs_cols[e, s, j * rows:(j + 1) * rows, :] = x[
                    pl.ds(2 * width + 16 + c0 + j, rows, stride=width), :].astype(BF16)
        return [remote(hs_cols.at[e, s], hr_cols.at[e, 1 - s],
                       hsend.at[e, 2 + s], hrcv.at[e, 2 + s], *around[2 + s]) for s in range(2)]

    in_x = (tx > 0, tx < gx - 1)
    in_y = (ty > 0, ty < gy - 1)

    def take_rows(e, x, cps):
        for cp in cps:
            cp.wait_recv()
        for s, r0 in ((0, 0), (1, rows + 2)):
            v = jnp.where(in_x[s], hr_rows[e, s].astype(F32), 0.0)
            for i in range(2):
                x[(r0 + i) * width + 16:(r0 + i) * width + 16 + cols, :] = v[i * cols:(i + 1) * cols]

    def take_rest(e, x, cps):
        for cp in cps:
            cp.wait_recv()
        for s, c0 in ((0, 14), (1, 16 + cols)):
            v = jnp.where(in_y[s], hr_cols[e, s].astype(F32), 0.0)
            for j in range(2):
                x[pl.ds(2 * width + c0 + j, rows, stride=width), :] = v[j * rows:(j + 1) * rows]
        q = 0
        for sr, r0 in ((0, 0), (1, rows + 2)):
            for sc, c0 in ((0, 14), (1, 16 + cols)):
                v = jnp.where(jnp.logical_and(in_x[sr], in_y[sc]),
                              hr_corner[e, q].astype(F32), 0.0)
                for i in range(2):
                    x[(r0 + i) * width + c0:(r0 + i) * width + c0 + 2, :] = v[2 * i:2 * i + 2]
                q += 1

    def widen(x, a, first, last, shift):
        for r in range(first, last):
            for dj in range(3):
                c = r * width + 15 + dj
                a[(r - shift) * cols:(r - shift + 1) * cols, dj * chans:(dj + 1) * chans] = x[
                    c:c + cols, :].astype(BF16)

    def widen_edge(x, a, first, last):
        for r in range(first, last):
            c = r * width + 15
            a[r * cols:r * cols + 16, 0:chans] = x[c:c + 16, :].astype(BF16)
            c = r * width + 17 + cols - 16
            a[(r + 1) * cols - 16:(r + 1) * cols, 2 * chans:3 * chans] = x[c:c + 16, :].astype(BF16)

    def widen_strip(x, s):
        for r in range(rows + 4):
            for dj in range(3):
                c = r * width + 15 + dj
                v = jnp.concatenate(
                    [x[c + cols - 4:c + cols + 4, :], x[c - 4:c + 4, :]], axis=0)
                s[r * 16:(r + 1) * 16, dj * chans:(dj + 1) * chans] = v.astype(BF16)

    def side(x, r, dj):
        c = (r + 2) * width + 15 + dj
        return jnp.concatenate([x[c:c + 8, :], x[c + cols - 8:c + cols, :]], axis=0)

    def widen_side(x, s):
        for r in range(1, rows - 1):
            for dj in range(3):
                s[(r - 1) * 16:r * 16, dj * chans:(dj + 1) * chans] = side(x, r, dj).astype(BF16)

    def conv_pairs(a, w2x, first, pairs):
        v = jnp.concatenate([
            jnp.concatenate([a[(first + 2 * p + d) * cols:(first + 2 * p + d + 1) * cols, :]
                             for p in range(pairs)], axis=0) for d in range(4)], axis=1)
        res = jnp.dot(v, w2x[...], preferred_element_type=F32)
        return [(first + 2 * p + s, res[p * cols:(p + 1) * cols, s * chans:(s + 1) * chans])
                for p in range(pairs) for s in range(2)]

    def conv_strip(s, w):
        v = jnp.concatenate([s[d * 16:(d + rows + 2) * 16, :] for d in range(3)], axis=1)
        return jnp.dot(v, w[...], preferred_element_type=F32)

    ld_cot.wait()
    fill(x_cot, cot_v)
    h_cot = rim_rows(0, x_cot, cot_v)
    h_cot2 = rim_cols(0, x_cot)

    third = 3 * chans
    ld_wb.wait()
    ld_wa.wait()
    for src, flip, two, two_flip in ((wb_v, wbt, w2_b, w2_bt), (wa_v, wat, w2_a, w2_at)):
        for t in range(9):
            flip[t * chans:(t + 1) * chans, :] = src[
                (8 - t) * chans:(9 - t) * chans, :].astype(F32).T.astype(BF16)
        for one, both in ((src, two), (flip, two_flip)):
            both[0:3 * third, 0:chans] = one[...]
            both[third:4 * third, chans:2 * chans] = one[...]
            both[3 * third:4 * third, 0:chans] = jnp.zeros((third, chans), BF16)
            both[0:third, chans:2 * chans] = jnp.zeros((third, chans), BF16)

    ld_raw.wait()
    step = px // 8

    def relay(i, _):
        rawf[...] = raw[pl.ds(pl.multiple_of(i * step * listed, 16), step * listed), :].astype(F32)
        for k in range(listed):
            interp2[pl.ds(pl.multiple_of(i * step, 16), step), k * cells:(k + 1) * cells] = rawf[
                pl.ds(k, step, stride=listed), :].astype(BF16)
        return 0
    lax.fori_loop(0, 8, relay, 0)

    ri = lax.broadcasted_iota(jnp.int32, (chans, chans), 0)
    ci = lax.broadcasted_iota(jnp.int32, (chans, chans), 1)
    half = chans // 2
    rest = ri % half
    perm = jnp.where(
        ci == (rest // span) * 2 * span + (ri // half) * span + rest % span, 1.0, 0.0).astype(BF16)

    def turn(v):
        return lax.dot_general(perm, v, NT, preferred_element_type=F32)

    lane = lax.broadcasted_iota(jnp.int32, (chans, (rows - 4) * cols), 1) % cols
    inner = jnp.logical_and(lane >= 2, lane < cols - 2)
    si = lax.broadcasted_iota(jnp.int32, (16, chans), 0)
    outer = jnp.logical_or(si < 2, si >= 14)

    def rows_and_sides(x):
        v = [x[(r + 2) * width + 16:(r + 2) * width + 16 + cols, :]
             for r in (0, 1, rows - 2, rows - 1)]
        v += [jnp.where(outer, side(x, r, 1), 0.0) for r in range(2, rows - 2)]
        return jnp.concatenate(v, axis=0).astype(BF16)

    cot_t[...] = jnp.where(
        inner, turn(cot_v[2 * cols:(rows - 2) * cols, :]), 0.0).astype(BF16)
    cot_r[...] = turn(rows_and_sides(x_cot)).astype(BF16)
    for x in (x_field, x_act):
        for r in range(2, rows + 2):
            x[r * width + 8:r * width + 16, :] = jnp.zeros((8, chans), F32)
            x[r * width + 16 + cols:r * width + 24 + cols, :] = jnp.zeros((8, chans), F32)

    for cp in ld_coarse:
        cp.wait()
    for cp in (l1[2], l1[3]):
        cp.wait_recv()
    ld_l = pltpu.make_async_copy(lrecv.at[pl.ds(2, 2)], lsm.at[pl.ds(2, 2)], lsem.at[0])
    ld_l.start()
    ld_l.wait()

    def clip(v):
        return jnp.minimum(jnp.maximum(v, 0), 2)

    ids = [lists[0, k] for k in range(listed)]
    wanted = [[lsm[i, k, 0] for k in range(listed)] for i in (2, 3)] + [ids]
    spots = [[(clip(i // (nb * gy) - tx + 1), i % nb) for i in row] for row in wanted]
    c2 = []
    for h, cut in enumerate(cuts):
        for cp in c1[h]:
            cp.wait_recv()
        for s in range(2):
            for k in range(listed):
                x, m = spots[s][k]
                picked[s, h, k] = calls[h][x, m]
            c2.append(remote(picked.at[s, h], crecv.at[1 - s, :, cut],
                             c2s.at[h, s], c2r.at[h, s], *around[2 + s]))
    for k in range(listed):
        x, m = spots[2][k]
        for h in range(PARTS):
            crecv[2, k, h * part:(h + 1) * part, :] = calls[h][x, m]

    for i in (0, 1, 4, 5, 6, 7):
        tell(i)
    take_rows(0, x_cot, h_cot[:2])
    take_rest(0, x_cot, h_cot[2:] + h_cot2)
    widen(x_cot, a_cot, 0, rows + 4, 0)
    widen_strip(x_cot, s_cot)
    for r, v in conv_pairs(a_cot, w2_bt, 0, (rows + 2) // 2):
        ba_main[r * cols:(r + 1) * cols, :] = v
    ba_strip[...] = conv_strip(s_cot, wbt)

    for cp in c2:
        cp.wait_recv()
    for k in range(listed):
        oy = (ids[k] // nb) % gy
        which = jnp.where(oy == ty, 2, jnp.where(oy < ty, 0, 1))
        bt[k * cells:(k + 1) * cells, :] = crecv[which, k].astype(F32).T.astype(BF16)
    ld_fine.wait()
    ld_lift.wait()

    def regrid(parts):
        def cut(ref):
            return jnp.concatenate([ref[p0 * cols:p1 * cols, :] for p0, p1 in parts], axis=0)
        g = jnp.dot(cut(interp2), bt[...], preferred_element_type=F32).astype(BF16)
        f = cut(fine_v).astype(F32) + jnp.dot(g, lift_v[...], preferred_element_type=F32)
        f = f.astype(BF16)
        o = 0
        for p0, p1 in parts:
            for r in range(p0, p1):
                v = f[o:o + cols]
                field[r * cols:(r + 1) * cols, :] = v
                x_field[(r + 2) * width + 16:(r + 2) * width + 16 + cols, :] = v.astype(F32)
                o += cols

    regrid(((0, 2), (rows - 2, rows)))
    h_rows = rim_rows(1, x_field, field)
    regrid(((2, rows - 2),))

    h_cols = rim_cols(1, x_field)
    widen(x_field, a_field, 2, rows + 2, 0)

    def point(pre, back):
        sig = 1.0 / (1.0 + jnp.exp(-pre))
        return pre * sig, back * (sig * (1.0 + pre * (1.0 - sig)))

    def keep(r, pre):
        act, bp = point(pre, ba_main[r * cols:(r + 1) * cols, :])
        c = (r + 1) * width + 16
        x_act[c:c + cols, :] = act
        x_bp[c:c + cols, :] = bp

    for r, pre in conv_pairs(a_field, w2_a, 2, (rows - 2) // 2):
        keep(r, pre)
    widen(x_act, a_act, 3, rows + 1, 1)

    def inner_grad(w, lhs, a, first):
        v = jnp.concatenate(
            [a[(first + d) * cols:(first + d + rows - 4) * cols, :] for d in range(3)], axis=1)
        wsum[w] = jnp.dot(lhs, v, preferred_element_type=F32)

    inner_grad(1, cot_t[...], a_act, 2)
    bp_in = jnp.concatenate([x_bp[(r + 2) * width + 16:(r + 2) * width + 16 + cols, :]
                             for r in range(2, rows - 2)], axis=0).astype(BF16)
    inner_grad(0, jnp.where(inner, turn(bp_in), 0.0).astype(BF16), a_field, 3)

    take_rows(1, x_field, h_rows[:2])
    widen(x_field, a_field, 0, 2, 0)
    widen(x_field, a_field, rows + 2, rows + 4, 0)
    for r0 in (0, rows):
        for r, pre in conv_pairs(a_field, w2_a, r0, 1):
            keep(r, pre)
    take_rest(1, x_field, h_cols + h_rows[2:])
    widen_edge(x_field, a_field, 1, 5)
    widen_edge(x_field, a_field, rows - 1, rows + 3)
    widen_strip(x_field, s_field)
    pre = conv_strip(s_field, wa_v)
    act, bp = point(pre, ba_strip[...])
    inside = lax.broadcasted_iota(jnp.int32, (8, chans), 0)
    far = jnp.logical_or(inside < 4, in_y[1])
    near = jnp.logical_or(inside >= 4, in_y[0])
    for x, v in ((x_act, act), (x_bp, bp)):
        for r in range(rows + 2):
            c = (r + 1) * width + 16
            x[c + cols - 4:c + cols + 4, :] = jnp.where(far, v[r * 16:r * 16 + 8], 0.0)
            x[c - 4:c + 4, :] = jnp.where(near, v[r * 16 + 8:r * 16 + 16], 0.0)

    for ok, r in ((in_x[0], 1), (in_x[1], rows + 2)):
        @pl.when(jnp.logical_not(ok))
        def _():
            for x in (x_act, x_bp):
                x[r * width:(r + 1) * width, :] = jnp.zeros((width, chans), F32)

    def weight_grad(w, lhs, a, first, sides):
        n = 2 * cols
        v = jnp.concatenate([
            jnp.concatenate([a[(first + d) * cols:(first + d) * cols + n, :],
                             a[(first + d + rows - 2) * cols:(first + d + rows - 2) * cols + n, :],
                             sides[d * 16:(d + rows - 4) * 16, :]], axis=0) for d in range(3)], axis=1)
        g = wsum[w] + jnp.dot(lhs, v, preferred_element_type=F32)
        wsum[w] = g
        wsend[w] = g.astype(BF16)

    def first(w):
        other = 1 - core
        return remote(wsend.at[w, pl.ds(pl.multiple_of(other * half, 16), half), :],
                      w1.at[w], wsnd.at[w, 0], wrcv.at[w, 0], mine * 2 + other, ty)

    def second(w, cp):
        own = wsum[w, pl.ds(pl.multiple_of(core * half, 16), half), :]
        cp.wait_recv()
        acc = own + w1[w].astype(F32)
        for s in range(sz.plane):
            parts = [acc[s * span:(s + 1) * span, g * third:(g + 1) * third] for g in range(3)]
            if sz.pack > 3 * span:
                parts.append(jnp.zeros((sz.pack - 3 * span, third), F32))
            wst2[w, s] = jnp.concatenate(parts, axis=0).astype(BF16)
        nxt = []
        for o in range(1, sz.plane):
            t = (mine + o) % sz.plane
            nxt.append(remote(wst2.at[w, t], w2.at[w, o - 1],
                              wsnd.at[w, o], wrcv.at[w, o], t * 2 + core, ty))
        return nxt

    def last(w, cps):
        acc = wst2[w, mine].astype(F32)
        for o, cp in enumerate(cps):
            cp.wait_recv()
            acc = acc + w2[w, o].astype(F32)
        w3[w, ty] = acc
        nxt = []
        for o in range(1, gy):
            j = sz.plane + o
            nxt.append(remote(w3.at[w, ty], w3.at[w, ty], wsnd.at[w, j], wrcv.at[w, j],
                              tx, (ty + o) % gy))
        return nxt

    def finish(w, cps, dst):
        for cp in cps:
            cp.wait_recv()
        acc = w3[w, 0]
        for z in range(1, gy):
            acc = acc + w3[w, z]
        for g in range(3):
            for u in range(3):
                dst[3 * g + u] = acc[g * span:(g + 1) * span, u * chans:(u + 1) * chans]

    widen(x_act, a_act, 1, 5, 1)
    widen(x_act, a_act, rows - 1, rows + 3, 1)
    widen_side(x_act, side_act)
    weight_grad(1, cot_r[...], a_act, 0, side_act)
    sb = first(1)
    widen_side(x_field, side_field)
    weight_grad(0, turn(rows_and_sides(x_bp)).astype(BF16), a_field, 1, side_field)
    sa = first(0)
    sb = second(1, sb)

    widen(x_bp, a_bp, 1, rows + 3, 1)
    bf = [(cot_v[r * cols:(r + 1) * cols, :].astype(F32) + v).astype(BF16)
          for r, v in conv_pairs(a_bp, w2_at, 0, rows // 2)]
    sa = second(0, sa)
    br = lax.dot_general(lift_v[...], jnp.concatenate(bf, axis=0), NT,
                         preferred_element_type=F32).astype(BF16)
    bb = jnp.dot(br, interp2[...], preferred_element_type=F32)
    for k in range(listed):
        v = bb[:, k * cells:(k + 1) * cells]
        gsum[k] = v
        gsend[k] = v.astype(BF16)
    d1 = [remote(gsend, g1.at[i ^ 1], gsnd.at[i], grcv.at[i], *around[i]) for i in range(8)]

    widen(x_act, a_act, 3, rows + 1, 1)
    for r, v in conv_pairs(a_act, w2_b, 0, rows // 2):
        q = slice(r * cols, (r + 1) * cols)
        out[q, :] = (field[q, :].astype(F32) + v).astype(BF16)

    for i in (0, 1, 4, 5, 6, 7):
        l1[i].wait_recv()
    ld_m = [pltpu.make_async_copy(lrecv.at[pl.ds(i, n)], lsm.at[pl.ds(i, n)], lsem.at[j])
            for j, (i, n) in ((1, (0, 2)), (2, (4, 4)))]
    for cp in ld_m:
        cp.start()
    for cp in ld_m:
        cp.wait()
    base = (tx * gy + ty) * nb

    def add(start, cand):
        def body(m, _):
            acc = start(m)
            for i, get in cand:
                acc = acc + jnp.where(i == base + m, get(), 0.0)
            gc[m] = acc
            return 0
        lax.fori_loop(0, nb, body, 0)

    def arrive(group):
        for s in group:
            d1[s].wait_recv()
        add(lambda m: gc[m], [(lsm[s, k, 0], lambda s=s, k=k: g1[s, k].astype(F32))
                              for s in group for k in range(listed)])

    add(lambda m: jnp.zeros((chans_in, cells), F32),
        [(ids[k], lambda k=k: gsum[k]) for k in range(listed)])
    sb = last(1, sb)
    arrive((0, 1))
    sa = last(0, sa)
    arrive((2, 3))
    arrive((4, 5, 6, 7))
    finish(1, sb, gb)
    finish(0, sa, ga)
    for cp in started:
        cp.wait_send()


def hand_out(*refs):
    count = (len(refs) - 1) // 2
    sems = refs[-1]
    copies = [pltpu.make_async_copy(refs[i], refs[count + i], sems.at[i]) for i in range(count)]
    for cp in copies:
        cp.start()
    for cp in copies:
        cp.wait()


def fused(sz, lists, coarse, interp, fine, lift, wa, wb, cot):
    rows, cols, chans, px, width = sz.rows, sz.cols, sz.chans, sz.px, sz.width
    nb, ci, cells, listed = sz.blocks, sz.chans_in, sz.cells, sz.listed
    vm = pltpu.VMEM
    dma = pltpu.SemaphoreType.DMA
    anyspace = pl.BlockSpec(memory_space=pl.ANY)
    vspace = pl.BlockSpec(memory_space=pltpu.VMEM)
    x = vm(((rows + 4) * width, chans), F32)
    a_ext = vm(((rows + 4) * cols, 3 * chans), BF16)
    strip = vm(((rows + 4) * 16, 3 * chans), BF16)
    a_main = vm(((rows + 2) * cols, 3 * chans), BF16)
    side = vm(((rows - 2) * 16, 3 * chans), BF16)
    w = vm((9 * chans, chans), BF16)
    w2 = vm((12 * chans, 2 * chans), BF16)
    scratch = [
        vm((3, nb, ci // PARTS, cells), BF16), vm((3, nb, ci // PARTS, cells), BF16),
        vm((8, 128), jnp.int32), vm((8, 8, 128), jnp.int32),
        pltpu.SMEM((8, 8, 128), jnp.int32), vm((2, PARTS, listed, ci // PARTS, cells), BF16),
        vm((3, listed, ci, cells), BF16),
        vm((px * listed, cells), BF16), vm((px * listed // 8, cells), F32),
        vm((px, listed * cells), BF16), vm((px, chans), BF16), vm((ci, chans), BF16),
        w, w, w, w, w2, w2, w2, w2,
        vm((px, chans), BF16), vm((listed * cells, ci), BF16),
        x, x, x, x, a_ext, a_ext, strip, strip, a_main, a_main, side, side,
        vm(((rows + 2) * cols, chans), F32), vm(((rows + 2) * 16, chans), F32),
        vm((px, chans), BF16), vm((px, chans), BF16),
        vm((chans, (rows - 4) * cols), BF16), vm((chans, 4 * cols + (rows - 4) * 16), BF16),
        vm((2, 2, 2 * rows, chans), BF16), vm((2, 4, 16, chans), BF16),
        vm((2, 2, 2 * cols, chans), BF16), vm((2, 2, 2 * rows, chans), BF16),
        vm((2, 4, 16, chans), BF16),
        vm((2, chans, 9 * chans), F32), vm((2, chans, 9 * chans), BF16),
        vm((2, chans // 2, 9 * chans), BF16),
        vm((2, sz.plane, sz.pack, 3 * chans), BF16),
        vm((2, sz.plane - 1, sz.pack, 3 * chans), BF16),
        vm((2, sz.gy, sz.pack, 3 * chans), F32),
        vm((listed, ci, cells), F32), vm((listed, ci, cells), BF16),
        vm((8, listed, ci, cells), BF16),
        dma((8,)), dma((3,)), dma((12,)), dma((12,)),
        dma((PARTS, 2)), dma((PARTS, 2)), dma((PARTS, 2)), dma((PARTS, 2)), dma((2, 8)), dma((2, 8)),
        dma((2, sz.plane + sz.gy)), dma((2, sz.plane + sz.gy)), dma((8,)), dma((8,)),
    ]
    flops = 2 * px * (6 * 9 * chans * chans + 2 * listed * cells * ci + 2 * ci * chans)
    shapes = (
        jax.ShapeDtypeStruct((px, chans), BF16),
        jax.ShapeDtypeStruct((9, sz.span, chans), F32),
        jax.ShapeDtypeStruct((9, sz.span, chans), F32),
        jax.ShapeDtypeStruct((nb, ci, cells), F32),
    )
    results = pl.pallas_call(
        functools.partial(kernel, sz),
        out_shape=tuple(pltpu.VMEM(v.shape, v.dtype) for v in shapes),
        in_specs=[pl.BlockSpec(memory_space=pltpu.SMEM)] + [anyspace] * 7,
        out_specs=(vspace, vspace, vspace, vspace),
        scratch_shapes=scratch,
        compiler_params=pltpu.CompilerParams(
            collective_id=0, has_side_effects=True, vmem_limit_bytes=56 * MIB),
        cost_estimate=pl.CostEstimate(flops=flops, bytes_accessed=5 * MIB, transcendentals=px * chans),
    )(lists, coarse, interp, fine, lift, wa, wb, cot)
    return pl.pallas_call(
        hand_out,
        out_shape=shapes,
        in_specs=[vspace] * 4,
        out_specs=(anyspace,) * 4,
        scratch_shapes=[dma((4,))],
        compiler_params=pltpu.CompilerParams(vmem_limit_bytes=4 * MIB),
    )(*results)


def on_device(nx, ny, coarse, lists, interp, fine_own, lift, conv_a, conv_b, cotangent):
    rows, cols, chans = fine_own.shape
    listed, cells = interp.shape[2:]
    blocks, chans_in = coarse.shape[2:4]
    sz = Sizes(lax.axis_size("gx"), lax.axis_size("gy"), nx, ny, rows, cols, chans, chans_in,
               cells, listed, blocks)
    output, ga, gb, gc = fused(
        sz,
        lists.reshape(1, listed),
        coarse.reshape(blocks, chans_in, cells),
        interp.reshape(rows * cols * listed, cells),
        fine_own.reshape(rows * cols, chans),
        lift,
        conv_a.reshape(9 * chans, chans),
        conv_b.reshape(9 * chans, chans),
        cotangent.reshape(rows * cols, chans),
    )
    return (
        output.reshape(rows, cols, chans),
        jnp.transpose(ga, (0, 2, 1)),
        jnp.transpose(gb, (0, 2, 1)),
        gc.reshape(1, 1, blocks, chans_in, cells),
    )


def solution(mesh):
    side = {32: 4, 8: 2}[mesh.shape["gx"]]
    placed = (
        P("gx", "gy", None, None, None),
        P("gx", "gy", None),
        P("gx", "gy", None, None),
        P("gx", "gy", None),
        P(),
        P(),
        P(),
        P("gx", "gy", None),
    )
    return jax.shard_map(
        functools.partial(on_device, side, side),
        mesh=mesh,
        in_specs=placed,
        out_specs=(
            P("gx", "gy", None),
            P(None, None, "gx"),
            P(None, None, "gx"),
            P("gx", "gy", None, None, None),
        ),
        check_vma=False,
    )
```

```python
import functools

import jax
import jax.numpy as jnp
from jax import lax
from jax.experimental import pallas as pl
from jax.experimental.pallas import tpu as pltpu
from jax.sharding import PartitionSpec as P

MESH = pl.DeviceIdType.MESH
F32 = jnp.float32
BF16 = jnp.bfloat16
MIB = 1024 * 1024
PARTS = 2
NT = (((1,), (1,)), ((), ()))
AROUND = ((-1, 0), (1, 0), (0, -1), (0, 1), (-1, -1), (1, 1), (-1, 1), (1, -1))


class Sizes:
    def __init__(self, gx, gy, nx, ny, rows, cols, chans, chans_in, cells, listed, blocks):
        self.gx, self.gy, self.nx, self.ny = gx, gy, nx, ny
        self.rows, self.cols = rows, cols
        self.chans, self.chans_in, self.cells = chans, chans_in, cells
        self.listed, self.blocks = listed, blocks
        self.px = rows * cols
        self.width = cols + 32
        self.span = chans // gx
        self.pack = -(-3 * self.span // 16) * 16
        self.plane = nx * ny


def kernel(
    sz,
    lists, coarse, interp, fine, lift, wa, wb, cot,
    out, ga, gb, gc,
    call0, call1, lvec, lrecv, lsm, picked, crecv,
    raw, rawf, interp2, fine_v, lift_v, wa_v, wb_v, wat, wbt, w2_a, w2_b, w2_at, w2_bt, cot_v, bt,
    x_cot, x_field, x_act, x_bp, a_cot, a_field, s_cot, s_field, a_act, a_bp,
    side_act, side_field, ba_main, ba_strip, field, out_v, cot_t, cot_r,
    hs_cols, hs_corner, hr_rows, hr_cols, hr_corner,
    wsum, wsend, w1, wst2, w2, w3,
    gsum, gsend, g1,
    local_sem, lsem, csend, crcv, c1s, c1r, c2s, c2r, hsend, hrcv, wsnd, wrcv, gsnd, grcv,
):
    tx = lax.axis_index("gx")
    ty = lax.axis_index("gy")
    gx, gy, nx, ny = sz.gx, sz.gy, sz.nx, sz.ny
    rows, cols, chans, width, px = sz.rows, sz.cols, sz.chans, sz.width, sz.px
    listed, cells, chans_in, nb, span = sz.listed, sz.cells, sz.chans_in, sz.blocks, sz.span
    core = tx % 2
    mine = tx // 2
    around = [((tx + dx + gx) % gx, (ty + dy + gy) % gy) for dx, dy in AROUND]
    started = []

    def remote(src, dst, ssem, rsem, px_, py_):
        copy = pltpu.make_async_remote_copy(
            src_ref=src, dst_ref=dst, send_sem=ssem, recv_sem=rsem,
            device_id=(px_, py_), device_id_type=MESH,
        )
        copy.start()
        started.append(copy)
        return copy

    def local(src, dst, i):
        copy = pltpu.make_async_copy(src, dst, local_sem.at[i])
        copy.start()
        return copy

    calls = (call0, call1)
    part = chans_in // PARTS
    cuts = [pl.ds(h * part, part) for h in range(PARTS)]
    ld_coarse = [local(coarse.at[:, cut], calls[h].at[1], 7 * h) for h, cut in enumerate(cuts)]
    ld_cot = local(cot, cot_v, 1)
    ld_wb = local(wb, wb_v, 3)
    ld_raw = local(interp, raw, 2)
    ld_wa = local(wa, wa_v, 4)
    ld_fine = local(fine, fine_v, 5)
    ld_lift = local(lift, lift_v, 6)

    peers = list(around)
    for o in range(2, gy - 1):
        peers.append((tx, (ty + o) % gy))
    for o in range(1, sz.plane):
        peers.append((((mine + o) % sz.plane) * 2 + core, ty))
    barrier = pltpu.get_barrier_semaphore()
    for p in peers:
        pl.semaphore_signal(barrier, inc=1, device_id=p, device_id_type=MESH)
    rowi = lax.broadcasted_iota(jnp.int32, (8, 128), 0)
    vec = jnp.zeros((8, 128), jnp.int32)
    for k in range(listed):
        vec = jnp.where(rowi == k, lists[0, k], vec)
    lvec[...] = vec

    def fill(x, src):
        for r in range(rows):
            x[(r + 2) * width + 16:(r + 2) * width + 16 + cols, :] = src[
                r * cols:(r + 1) * cols].astype(F32)

    pl.semaphore_wait(barrier, len(peers))

    l1 = {}

    def tell(i):
        l1[i] = remote(lvec, lrecv.at[i ^ 1], csend.at[4 + i], crcv.at[4 + i], *around[i])

    tell(2)
    tell(3)
    c1 = [[remote(coarse.at[:, cut], calls[h].at[2 - 2 * i], c1s.at[h, i], c1r.at[h, i], *around[i])
           for i in range(2)] for h, cut in enumerate(cuts)]

    def rim_rows(e, x, main):
        n2 = 2 * cols
        corners = []
        q = 0
        for r0, i0 in ((0, (4, 6)), (rows - 2, (7, 5))):
            for c0, i in ((0, i0[0]), (cols - 2, i0[1])):
                parts = [x[(2 + r0 + k) * width + 16 + c0:(2 + r0 + k) * width + 18 + c0, :]
                         for k in range(2)]
                parts.append(jnp.zeros((12, chans), F32))
                hs_corner[e, q] = jnp.concatenate(parts, axis=0).astype(BF16)
                corners.append(remote(hs_corner.at[e, q], hr_corner.at[e, 3 - q],
                                      hsend.at[e, 4 + q], hrcv.at[e, 4 + q], *around[i]))
                q += 1
        return [remote(main.at[pl.ds(0, n2), :], hr_rows.at[e, 1],
                       hsend.at[e, 0], hrcv.at[e, 0], *around[0]),
                remote(main.at[pl.ds(px - n2, n2), :], hr_rows.at[e, 0],
                       hsend.at[e, 1], hrcv.at[e, 1], *around[1])] + corners

    def rim_cols(e, x):
        for s, c0 in ((0, 0), (1, cols - 2)):
            for j in range(2):
                hs_cols[e, s, j * rows:(j + 1) * rows, :] = x[
                    pl.ds(2 * width + 16 + c0 + j, rows, stride=width), :].astype(BF16)
        return [remote(hs_cols.at[e, s], hr_cols.at[e, 1 - s],
                       hsend.at[e, 2 + s], hrcv.at[e, 2 + s], *around[2 + s]) for s in range(2)]

    in_x = (tx > 0, tx < gx - 1)
    in_y = (ty > 0, ty < gy - 1)

    def take_rows(e, x, cps):
        for cp in cps:
            cp.wait_recv()
        for s, r0 in ((0, 0), (1, rows + 2)):
            v = jnp.where(in_x[s], hr_rows[e, s].astype(F32), 0.0)
            for i in range(2):
                x[(r0 + i) * width + 16:(r0 + i) * width + 16 + cols, :] = v[i * cols:(i + 1) * cols]

    def take_rest(e, x, cps):
        for cp in cps:
            cp.wait_recv()
        for s, c0 in ((0, 14), (1, 16 + cols)):
            v = jnp.where(in_y[s], hr_cols[e, s].astype(F32), 0.0)
            for j in range(2):
                x[pl.ds(2 * width + c0 + j, rows, stride=width), :] = v[j * rows:(j + 1) * rows]
        q = 0
        for sr, r0 in ((0, 0), (1, rows + 2)):
            for sc, c0 in ((0, 14), (1, 16 + cols)):
                v = jnp.where(jnp.logical_and(in_x[sr], in_y[sc]),
                              hr_corner[e, q].astype(F32), 0.0)
                for i in range(2):
                    x[(r0 + i) * width + c0:(r0 + i) * width + c0 + 2, :] = v[2 * i:2 * i + 2]
                q += 1

    def widen(x, a, first, last, shift):
        for r in range(first, last):
            for dj in range(3):
                c = r * width + 15 + dj
                a[(r - shift) * cols:(r - shift + 1) * cols, dj * chans:(dj + 1) * chans] = x[
                    c:c + cols, :].astype(BF16)

    def widen_edge(x, a, first, last):
        for r in range(first, last):
            c = r * width + 15
            a[r * cols:r * cols + 16, 0:chans] = x[c:c + 16, :].astype(BF16)
            c = r * width + 17 + cols - 16
            a[(r + 1) * cols - 16:(r + 1) * cols, 2 * chans:3 * chans] = x[c:c + 16, :].astype(BF16)

    def widen_strip(x, s):
        for r in range(rows + 4):
            for dj in range(3):
                c = r * width + 15 + dj
                v = jnp.concatenate(
                    [x[c + cols - 4:c + cols + 4, :], x[c - 4:c + 4, :]], axis=0)
                s[r * 16:(r + 1) * 16, dj * chans:(dj + 1) * chans] = v.astype(BF16)

    def side(x, r, dj):
        c = (r + 2) * width + 15 + dj
        return jnp.concatenate([x[c:c + 8, :], x[c + cols - 8:c + cols, :]], axis=0)

    def widen_side(x, s):
        for r in range(1, rows - 1):
            for dj in range(3):
                s[(r - 1) * 16:r * 16, dj * chans:(dj + 1) * chans] = side(x, r, dj).astype(BF16)

    def conv_pairs(a, w2x, first, pairs):
        v = jnp.concatenate([
            jnp.concatenate([a[(first + 2 * p + d) * cols:(first + 2 * p + d + 1) * cols, :]
                             for p in range(pairs)], axis=0) for d in range(4)], axis=1)
        res = jnp.dot(v, w2x[...], preferred_element_type=F32)
        return [(first + 2 * p + s, res[p * cols:(p + 1) * cols, s * chans:(s + 1) * chans])
                for p in range(pairs) for s in range(2)]

    def conv_strip(s, w):
        v = jnp.concatenate([s[d * 16:(d + rows + 2) * 16, :] for d in range(3)], axis=1)
        return jnp.dot(v, w[...], preferred_element_type=F32)

    ld_cot.wait()
    fill(x_cot, cot_v)
    h_cot = rim_rows(0, x_cot, cot_v)
    h_cot2 = rim_cols(0, x_cot)

    third = 3 * chans
    ld_wb.wait()
    ld_wa.wait()
    for src, flip, two, two_flip in ((wb_v, wbt, w2_b, w2_bt), (wa_v, wat, w2_a, w2_at)):
        for t in range(9):
            flip[t * chans:(t + 1) * chans, :] = src[
                (8 - t) * chans:(9 - t) * chans, :].astype(F32).T.astype(BF16)
        for one, both in ((src, two), (flip, two_flip)):
            both[0:3 * third, 0:chans] = one[...]
            both[third:4 * third, chans:2 * chans] = one[...]
            both[3 * third:4 * third, 0:chans] = jnp.zeros((third, chans), BF16)
            both[0:third, chans:2 * chans] = jnp.zeros((third, chans), BF16)

    ld_raw.wait()
    step = px // 8

    def relay(i, _):
        rawf[...] = raw[pl.ds(pl.multiple_of(i * step * listed, 16), step * listed), :].astype(F32)
        for k in range(listed):
            interp2[pl.ds(pl.multiple_of(i * step, 16), step), k * cells:(k + 1) * cells] = rawf[
                pl.ds(k, step, stride=listed), :].astype(BF16)
        return 0
    lax.fori_loop(0, 8, relay, 0)

    ri = lax.broadcasted_iota(jnp.int32, (chans, chans), 0)
    ci = lax.broadcasted_iota(jnp.int32, (chans, chans), 1)
    half = chans // 2
    rest = ri % half
    perm = jnp.where(
        ci == (rest // span) * 2 * span + (ri // half) * span + rest % span, 1.0, 0.0).astype(BF16)

    def turn(v):
        return lax.dot_general(perm, v, NT, preferred_element_type=F32)

    lane = lax.broadcasted_iota(jnp.int32, (chans, (rows - 4) * cols), 1) % cols
    inner = jnp.logical_and(lane >= 2, lane < cols - 2)
    si = lax.broadcasted_iota(jnp.int32, (16, chans), 0)
    outer = jnp.logical_or(si < 2, si >= 14)

    def rows_and_sides(x):
        v = [x[(r + 2) * width + 16:(r + 2) * width + 16 + cols, :]
             for r in (0, 1, rows - 2, rows - 1)]
        v += [jnp.where(outer, side(x, r, 1), 0.0) for r in range(2, rows - 2)]
        return jnp.concatenate(v, axis=0).astype(BF16)

    cot_t[...] = jnp.where(
        inner, turn(cot_v[2 * cols:(rows - 2) * cols, :]), 0.0).astype(BF16)
    cot_r[...] = turn(rows_and_sides(x_cot)).astype(BF16)
    for x in (x_cot, x_field, x_act):
        for r in range(2, rows + 2):
            x[r * width + 8:r * width + 16, :] = jnp.zeros((8, chans), F32)
            x[r * width + 16 + cols:r * width + 24 + cols, :] = jnp.zeros((8, chans), F32)

    def back(first, pairs):
        for r, v in conv_pairs(a_cot, w2_bt, first, pairs):
            ba_main[r * cols:(r + 1) * cols, :] = v

    widen(x_cot, a_cot, 2, rows + 2, 0)
    back(2, (rows - 2) // 2)

    for cp in ld_coarse:
        cp.wait()
    for cp in (l1[2], l1[3]):
        cp.wait_recv()
    ld_l = pltpu.make_async_copy(lrecv.at[pl.ds(2, 2)], lsm.at[pl.ds(2, 2)], lsem.at[0])
    ld_l.start()
    ld_l.wait()

    def clip(v):
        return jnp.minimum(jnp.maximum(v, 0), 2)

    ids = [lists[0, k] for k in range(listed)]
    wanted = [[lsm[i, k, 0] for k in range(listed)] for i in (2, 3)] + [ids]
    spots = [[(clip(i // (nb * gy) - tx + 1), i % nb) for i in row] for row in wanted]
    c2 = []
    for h, cut in enumerate(cuts):
        for cp in c1[h]:
            cp.wait_recv()
        for s in range(2):
            for k in range(listed):
                x, m = spots[s][k]
                picked[s, h, k] = calls[h][x, m]
            c2.append(remote(picked.at[s, h], crecv.at[1 - s, :, cut],
                             c2s.at[h, s], c2r.at[h, s], *around[2 + s]))
    for k in range(listed):
        x, m = spots[2][k]
        for h in range(PARTS):
            crecv[2, k, h * part:(h + 1) * part, :] = calls[h][x, m]

    for i in (0, 1, 4, 5, 6, 7):
        tell(i)
    take_rows(0, x_cot, h_cot[:2])
    widen(x_cot, a_cot, 0, 2, 0)
    widen(x_cot, a_cot, rows + 2, rows + 4, 0)
    back(0, 1)
    back(rows, 1)
    take_rest(0, x_cot, h_cot[2:] + h_cot2)
    widen_strip(x_cot, s_cot)
    ba_strip[...] = conv_strip(s_cot, wbt)

    for cp in c2:
        cp.wait_recv()
    for k in range(listed):
        oy = (ids[k] // nb) % gy
        which = jnp.where(oy == ty, 2, jnp.where(oy < ty, 0, 1))
        bt[k * cells:(k + 1) * cells, :] = crecv[which, k].astype(F32).T.astype(BF16)
    ld_fine.wait()
    ld_lift.wait()

    def regrid(parts):
        def cut(ref):
            return jnp.concatenate([ref[p0 * cols:p1 * cols, :] for p0, p1 in parts], axis=0)
        g = jnp.dot(cut(interp2), bt[...], preferred_element_type=F32).astype(BF16)
        f = cut(fine_v).astype(F32) + jnp.dot(g, lift_v[...], preferred_element_type=F32)
        f = f.astype(BF16)
        o = 0
        for p0, p1 in parts:
            for r in range(p0, p1):
                v = f[o:o + cols]
                field[r * cols:(r + 1) * cols, :] = v
                x_field[(r + 2) * width + 16:(r + 2) * width + 16 + cols, :] = v.astype(F32)
                o += cols

    regrid(((0, 2), (rows - 2, rows)))
    h_rows = rim_rows(1, x_field, field)
    regrid(((2, rows - 2),))

    h_cols = rim_cols(1, x_field)
    widen(x_field, a_field, 2, rows + 2, 0)

    def point(pre, back):
        sig = 0.5 + 0.5 * jnp.tanh(0.5 * pre)
        return pre * sig, back * (sig * (1.0 + pre * (1.0 - sig)))

    def keep(r, pre):
        act, bp = point(pre, ba_main[r * cols:(r + 1) * cols, :])
        c = (r + 1) * width + 16
        x_act[c:c + cols, :] = act
        x_bp[c:c + cols, :] = bp

    for r, pre in conv_pairs(a_field, w2_a, 2, (rows - 2) // 2):
        keep(r, pre)
    widen(x_act, a_act, 3, rows + 1, 1)

    def inner_grad(w, lhs, a, first):
        v = jnp.concatenate(
            [a[(first + d) * cols:(first + d + rows - 4) * cols, :] for d in range(3)], axis=1)
        wsum[w] = jnp.dot(lhs, v, preferred_element_type=F32)

    inner_grad(1, cot_t[...], a_act, 2)
    bp_in = jnp.concatenate([x_bp[(r + 2) * width + 16:(r + 2) * width + 16 + cols, :]
                             for r in range(2, rows - 2)], axis=0).astype(BF16)
    inner_grad(0, jnp.where(inner, turn(bp_in), 0.0).astype(BF16), a_field, 3)

    take_rows(1, x_field, h_rows[:2])
    widen(x_field, a_field, 0, 2, 0)
    widen(x_field, a_field, rows + 2, rows + 4, 0)
    for r0 in (0, rows):
        for r, pre in conv_pairs(a_field, w2_a, r0, 1):
            keep(r, pre)
    take_rest(1, x_field, h_cols + h_rows[2:])
    widen_edge(x_field, a_field, 1, 5)
    widen_edge(x_field, a_field, rows - 1, rows + 3)
    widen_strip(x_field, s_field)
    pre = conv_strip(s_field, wa_v)
    act, bp = point(pre, ba_strip[...])
    inside = lax.broadcasted_iota(jnp.int32, (8, chans), 0)
    far = jnp.logical_or(inside < 4, in_y[1])
    near = jnp.logical_or(inside >= 4, in_y[0])
    for x, v in ((x_act, act), (x_bp, bp)):
        for r in range(rows + 2):
            c = (r + 1) * width + 16
            x[c + cols - 4:c + cols + 4, :] = jnp.where(far, v[r * 16:r * 16 + 8], 0.0)
            x[c - 4:c + 4, :] = jnp.where(near, v[r * 16 + 8:r * 16 + 16], 0.0)

    for ok, r in ((in_x[0], 1), (in_x[1], rows + 2)):
        @pl.when(jnp.logical_not(ok))
        def _():
            for x in (x_act, x_bp):
                x[r * width:(r + 1) * width, :] = jnp.zeros((width, chans), F32)

    def weight_grad(w, lhs, a, first, sides):
        n = 2 * cols
        v = jnp.concatenate([
            jnp.concatenate([a[(first + d) * cols:(first + d) * cols + n, :],
                             a[(first + d + rows - 2) * cols:(first + d + rows - 2) * cols + n, :],
                             sides[d * 16:(d + rows - 4) * 16, :]], axis=0) for d in range(3)], axis=1)
        g = wsum[w] + jnp.dot(lhs, v, preferred_element_type=F32)
        wsum[w] = g
        wsend[w] = g.astype(BF16)

    def first(w):
        other = 1 - core
        return remote(wsend.at[w, pl.ds(pl.multiple_of(other * half, 16), half), :],
                      w1.at[w], wsnd.at[w, 0], wrcv.at[w, 0], mine * 2 + other, ty)

    def second(w, cp):
        own = wsum[w, pl.ds(pl.multiple_of(core * half, 16), half), :]
        cp.wait_recv()
        acc = own + w1[w].astype(F32)
        for s in range(sz.plane):
            parts = [acc[s * span:(s + 1) * span, g * third:(g + 1) * third] for g in range(3)]
            if sz.pack > 3 * span:
                parts.append(jnp.zeros((sz.pack - 3 * span, third), F32))
            wst2[w, s] = jnp.concatenate(parts, axis=0).astype(BF16)
        nxt = []
        for o in range(1, sz.plane):
            t = (mine + o) % sz.plane
            nxt.append(remote(wst2.at[w, t], w2.at[w, o - 1],
                              wsnd.at[w, o], wrcv.at[w, o], t * 2 + core, ty))
        return nxt

    def last(w, cps):
        acc = wst2[w, mine].astype(F32)
        for o, cp in enumerate(cps):
            cp.wait_recv()
            acc = acc + w2[w, o].astype(F32)
        w3[w, ty] = acc
        nxt = []
        for o in range(1, gy):
            j = sz.plane + o
            nxt.append(remote(w3.at[w, ty], w3.at[w, ty], wsnd.at[w, j], wrcv.at[w, j],
                              tx, (ty + o) % gy))
        return nxt

    def finish(w, cps, dst):
        for cp in cps:
            cp.wait_recv()
        acc = w3[w, 0]
        for z in range(1, gy):
            acc = acc + w3[w, z]
        for g in range(3):
            for u in range(3):
                dst[3 * g + u] = acc[g * span:(g + 1) * span, u * chans:(u + 1) * chans]

    widen(x_act, a_act, 1, 5, 1)
    widen(x_act, a_act, rows - 1, rows + 3, 1)
    widen_side(x_act, side_act)
    weight_grad(1, cot_r[...], a_act, 0, side_act)
    sb = first(1)
    widen_side(x_field, side_field)
    weight_grad(0, turn(rows_and_sides(x_bp)).astype(BF16), a_field, 1, side_field)
    sa = first(0)
    sb = second(1, sb)

    widen(x_bp, a_bp, 1, rows + 3, 1)
    def back_rows(first):
        return [(cot_v[r * cols:(r + 1) * cols, :].astype(F32) + v).astype(BF16)
                for r, v in conv_pairs(a_bp, w2_at, first, rows // 4)]

    bf = back_rows(0)
    sa = second(0, sa)
    bf += back_rows(rows // 2)
    br = lax.dot_general(lift_v[...], jnp.concatenate(bf, axis=0), NT,
                         preferred_element_type=F32).astype(BF16)
    bb = jnp.dot(br, interp2[...], preferred_element_type=F32)
    for k in range(listed):
        v = bb[:, k * cells:(k + 1) * cells]
        gsum[k] = v
        gsend[k] = v.astype(BF16)
    d1 = [remote(gsend, g1.at[i ^ 1], gsnd.at[i], grcv.at[i], *around[i]) for i in range(8)]

    widen(x_act, a_act, 3, rows + 1, 1)
    for r, v in conv_pairs(a_act, w2_b, 0, rows // 2):
        q = slice(r * cols, (r + 1) * cols)
        out[q, :] = (field[q, :].astype(F32) + v).astype(BF16)

    for i in (0, 1, 4, 5, 6, 7):
        l1[i].wait_recv()
    ld_m = [pltpu.make_async_copy(lrecv.at[pl.ds(i, n)], lsm.at[pl.ds(i, n)], lsem.at[j])
            for j, (i, n) in ((1, (0, 2)), (2, (4, 4)))]
    for cp in ld_m:
        cp.start()
    for cp in ld_m:
        cp.wait()
    base = (tx * gy + ty) * nb

    def add(start, cand):
        def body(m, _):
            acc = start(m)
            for i, get in cand:
                acc = acc + jnp.where(i == base + m, get(), 0.0)
            gc[m] = acc
            return 0
        lax.fori_loop(0, nb, body, 0)

    def arrive(group):
        for s in group:
            d1[s].wait_recv()
        add(lambda m: gc[m], [(lsm[s, k, 0], lambda s=s, k=k: g1[s, k].astype(F32))
                              for s in group for k in range(listed)])

    add(lambda m: jnp.zeros((chans_in, cells), F32),
        [(ids[k], lambda k=k: gsum[k]) for k in range(listed)])
    sb = last(1, sb)
    arrive((0, 1))
    sa = last(0, sa)
    arrive((2, 3))
    arrive((4, 5, 6, 7))
    finish(1, sb, gb)
    finish(0, sa, ga)
    for cp in started:
        cp.wait_send()


def hand_out(*refs):
    count = (len(refs) - 1) // 2
    sems = refs[-1]
    copies = [pltpu.make_async_copy(refs[i], refs[count + i], sems.at[i]) for i in range(count)]
    for cp in copies:
        cp.start()
    for cp in copies:
        cp.wait()


def fused(sz, lists, coarse, interp, fine, lift, wa, wb, cot):
    rows, cols, chans, px, width = sz.rows, sz.cols, sz.chans, sz.px, sz.width
    nb, ci, cells, listed = sz.blocks, sz.chans_in, sz.cells, sz.listed
    vm = pltpu.VMEM
    dma = pltpu.SemaphoreType.DMA
    anyspace = pl.BlockSpec(memory_space=pl.ANY)
    vspace = pl.BlockSpec(memory_space=pltpu.VMEM)
    x = vm(((rows + 4) * width, chans), F32)
    a_ext = vm(((rows + 4) * cols, 3 * chans), BF16)
    strip = vm(((rows + 4) * 16, 3 * chans), BF16)
    a_main = vm(((rows + 2) * cols, 3 * chans), BF16)
    side = vm(((rows - 2) * 16, 3 * chans), BF16)
    w = vm((9 * chans, chans), BF16)
    w2 = vm((12 * chans, 2 * chans), BF16)
    scratch = [
        vm((3, nb, ci // PARTS, cells), BF16), vm((3, nb, ci // PARTS, cells), BF16),
        vm((8, 128), jnp.int32), vm((8, 8, 128), jnp.int32),
        pltpu.SMEM((8, 8, 128), jnp.int32), vm((2, PARTS, listed, ci // PARTS, cells), BF16),
        vm((3, listed, ci, cells), BF16),
        vm((px * listed, cells), BF16), vm((px * listed // 8, cells), F32),
        vm((px, listed * cells), BF16), vm((px, chans), BF16), vm((ci, chans), BF16),
        w, w, w, w, w2, w2, w2, w2,
        vm((px, chans), BF16), vm((listed * cells, ci), BF16),
        x, x, x, x, a_ext, a_ext, strip, strip, a_main, a_main, side, side,
        vm(((rows + 2) * cols, chans), F32), vm(((rows + 2) * 16, chans), F32),
        vm((px, chans), BF16), vm((px, chans), BF16),
        vm((chans, (rows - 4) * cols), BF16), vm((chans, 4 * cols + (rows - 4) * 16), BF16),
        vm((2, 2, 2 * rows, chans), BF16), vm((2, 4, 16, chans), BF16),
        vm((2, 2, 2 * cols, chans), BF16), vm((2, 2, 2 * rows, chans), BF16),
        vm((2, 4, 16, chans), BF16),
        vm((2, chans, 9 * chans), F32), vm((2, chans, 9 * chans), BF16),
        vm((2, chans // 2, 9 * chans), BF16),
        vm((2, sz.plane, sz.pack, 3 * chans), BF16),
        vm((2, sz.plane - 1, sz.pack, 3 * chans), BF16),
        vm((2, sz.gy, sz.pack, 3 * chans), F32),
        vm((listed, ci, cells), F32), vm((listed, ci, cells), BF16),
        vm((8, listed, ci, cells), BF16),
        dma((8,)), dma((3,)), dma((12,)), dma((12,)),
        dma((PARTS, 2)), dma((PARTS, 2)), dma((PARTS, 2)), dma((PARTS, 2)), dma((2, 8)), dma((2, 8)),
        dma((2, sz.plane + sz.gy)), dma((2, sz.plane + sz.gy)), dma((8,)), dma((8,)),
    ]
    flops = 2 * px * (6 * 9 * chans * chans + 2 * listed * cells * ci + 2 * ci * chans)
    shapes = (
        jax.ShapeDtypeStruct((px, chans), BF16),
        jax.ShapeDtypeStruct((9, sz.span, chans), F32),
        jax.ShapeDtypeStruct((9, sz.span, chans), F32),
        jax.ShapeDtypeStruct((nb, ci, cells), F32),
    )
    results = pl.pallas_call(
        functools.partial(kernel, sz),
        out_shape=tuple(pltpu.VMEM(v.shape, v.dtype) for v in shapes),
        in_specs=[pl.BlockSpec(memory_space=pltpu.SMEM)] + [anyspace] * 7,
        out_specs=(vspace, vspace, vspace, vspace),
        scratch_shapes=scratch,
        compiler_params=pltpu.CompilerParams(
            collective_id=0, has_side_effects=True, vmem_limit_bytes=56 * MIB),
        cost_estimate=pl.CostEstimate(flops=flops, bytes_accessed=5 * MIB, transcendentals=px * chans),
    )(lists, coarse, interp, fine, lift, wa, wb, cot)
    return pl.pallas_call(
        hand_out,
        out_shape=shapes,
        in_specs=[vspace] * 4,
        out_specs=(anyspace,) * 4,
        scratch_shapes=[dma((4,))],
        compiler_params=pltpu.CompilerParams(vmem_limit_bytes=4 * MIB),
    )(*results)


def on_device(nx, ny, coarse, lists, interp, fine_own, lift, conv_a, conv_b, cotangent):
    rows, cols, chans = fine_own.shape
    listed, cells = interp.shape[2:]
    blocks, chans_in = coarse.shape[2:4]
    sz = Sizes(lax.axis_size("gx"), lax.axis_size("gy"), nx, ny, rows, cols, chans, chans_in,
               cells, listed, blocks)
    output, ga, gb, gc = fused(
        sz,
        lists.reshape(1, listed),
        coarse.reshape(blocks, chans_in, cells),
        interp.reshape(rows * cols * listed, cells),
        fine_own.reshape(rows * cols, chans),
        lift,
        conv_a.reshape(9 * chans, chans),
        conv_b.reshape(9 * chans, chans),
        cotangent.reshape(rows * cols, chans),
    )
    return (
        output.reshape(rows, cols, chans),
        jnp.transpose(ga, (0, 2, 1)),
        jnp.transpose(gb, (0, 2, 1)),
        gc.reshape(1, 1, blocks, chans_in, cells),
    )


def solution(mesh):
    side = {32: 4, 8: 2}[mesh.shape["gx"]]
    placed = (
        P("gx", "gy", None, None, None),
        P("gx", "gy", None),
        P("gx", "gy", None, None),
        P("gx", "gy", None),
        P(),
        P(),
        P(),
        P("gx", "gy", None),
    )
    return jax.shard_map(
        functools.partial(on_device, side, side),
        mesh=mesh,
        in_specs=placed,
        out_specs=(
            P("gx", "gy", None),
            P(None, None, "gx"),
            P(None, None, "gx"),
            P("gx", "gy", None, None, None),
        ),
        check_vma=False,
    )
```
